32 devices in a mesh: loop: 8 (over y, x, core), tp: 4 (over z).
Axes of the slice: x: 2, y: 2, z: 4, core: 2. Of those that a mesh axis runs over, the one named last changes fastest.
Arguments:
- queries: bfloat16 [2048, 4096], P('loop', 'tp'), may hold values from -8 to 8
- key_values: bfloat16 [2048, 1024], P('loop', 'tp'), may hold values from -8 to 8
- prompt_ids: int32 [2048], P('loop'), may hold values from 0 to 3, never falling along the last dimension, each value on 1 to 1024 neighbouring positions
- out_weight: bfloat16 [4096, 4096], P('tp'), may hold values from -5 to 5
Outputs:
- mixed: bfloat16 [2048, 4096], P('loop', 'tp')
The draws below stay inside these ranges and needn't reach their ends.
Inputs may be any that keep to these rules, and one draw needn't show every extreme that they name: `prompt_ids`: prompt numbers never fall along the tokens; each prompt holds 1 to 1024 tokens and one holds exactly 1024.
All inputs are finite; a program needn't handle non-finite values.
Results may differ from the reference program's by a relative error of at most 0.018.
Values may be sent and summed in bfloat16 or wider, within the bound.
A program may use at most 64 MiB of HBM per device.

```python
import math
import jax
import jax.numpy as jnp
import numpy as np
from jax import lax

HD = 128
GROUP = 8
D_OUT = 4096
STRETCH = 256
KV_HEADS = 4
Q_HEADS = 32
TOKENS = 2048
SPAN = 4
MOST = 1024
PROMPTS = 4
N_LOOP = 8
N_TP = 4


def draw_queries(key, part):
    key = jax.random.fold_in(key, 11)
    drawn_values = jnp.clip(jax.random.normal(key, (TOKENS, KV_HEADS * GROUP * HD), jnp.float32), -8.0, 8.0)
    return drawn_values.astype(jnp.bfloat16)


def draw_key_values(key, part):
    key = jax.random.fold_in(key, 12)
    drawn_values = jnp.clip(jax.random.normal(key, (TOKENS, KV_HEADS, 2, HD), jnp.float32), -8.0, 8.0)
    return drawn_values.reshape(TOKENS, KV_HEADS * 2 * HD).astype(jnp.bfloat16)


def raised(drawn, own_key, source, target, parts, factor):
    owner, partner = [(jnp.arange(drawn.shape[axis_at]) // (drawn.shape[axis_at] // parts)).reshape([-1 if axis == axis_at else 1 for axis in range(drawn.ndim)]) for axis_at in (source, target)]
    chosen = jax.random.permutation(own_key, parts)[partner]
    strong = (owner == chosen) | (owner == (partner + parts // 2) % parts)
    return jnp.where(strong, factor * drawn, drawn)


def levels(key, shape, split, least, high):
    level = 1.0
    for axis_at, parts in split:
        heights = jax.random.uniform(jax.random.fold_in(jax.random.fold_in(key, 6), axis_at), (parts,), jnp.float32, least / len(split), high / len(split))
        level = level * jnp.repeat(jnp.exp(heights), shape[axis_at] // parts).reshape((-1,) + (1,) * (len(shape) - 1 - axis_at))
    return level


def length_profile(number_of, total, reach, skew):
    loads = [(1 << 20) // math.isqrt(rank ** skew) + 1 for rank in range(2, number_of + 1)]
    surplus, given = total - reach - (number_of - 1), [1] * (number_of - 1)
    while surplus > 0:
        candidates = [i for i in range(number_of - 1) if given[i] < reach]
        whole, left = sum([loads[i] for i in candidates]), surplus
        for i in candidates:
            extra = min(reach - given[i], max(1, left * loads[i] // whole), surplus)
            given[i] = given[i] + extra
            surplus = surplus - extra
    return np.array([reach] + given)


def ragged_sizes(own_key, number_of, total, most, slope):
    if number_of == 2:
        one = jax.random.randint(own_key, (), max(1, total - most), min(most, total - 1) + 1)
        return jnp.stack([one, total - one])
    lengths = jnp.asarray(length_profile(number_of, total, most, slope), jnp.int32)
    pairs = (number_of - 1) // 2
    source_of, taker = lengths[1:1 + 2 * pairs:2], lengths[2:2 + 2 * pairs:2]
    room = jnp.minimum(source_of - 1, most - taker)
    moved = jax.random.randint(jax.random.fold_in(own_key, 1), (pairs,), 0, 1 << 20) % (room + 1)
    lengths = lengths.at[1:1 + 2 * pairs:2].set(source_of - moved).at[2:2 + 2 * pairs:2].set(taker + moved)
    return lengths[jax.random.permutation(jax.random.fold_in(own_key, 2), number_of)]


def noise_with(stream_key, extent, deviation, most, shards, heavy, held_as=jnp.bfloat16):
    values = deviation * jax.random.normal(stream_key, extent, jnp.float32)
    if shards:
        values = values * levels(stream_key, extent, shards, -0.22, 0.18)
    return jnp.clip(raised(values, jax.random.fold_in(stream_key, 3), *heavy), -most, most).astype(held_as)


def setup_inputs(seed: int = 0) -> dict:
    arg_keys = jax.random.split(jax.random.key(seed), 5)
    return {
        "queries": draw_queries(jax.random.fold_in(arg_keys[4], 71), 0),
        "key_values": draw_key_values(jax.random.fold_in(arg_keys[4], 71), 0),
        "prompt_ids": jnp.searchsorted(jnp.cumsum(ragged_sizes(arg_keys[2], PROMPTS, TOKENS, MOST, 1)), jnp.arange(TOKENS), side="right").astype(jnp.int32),
        "out_weight": noise_with(arg_keys[3], (Q_HEADS * HD, D_OUT), 0.25, 5.0, ((0, 4),), (0, 1, 4, 2.0)),
    }


masked_score = -1e+30

def reference(queries, key_values, prompt_ids, out_weight):
    pad_rows = SPAN * STRETCH
    paired = key_values.reshape(TOKENS, KV_HEADS, 2, HD)
    padded_keys = jnp.pad(paired[:, :, 0, :], ((pad_rows, 0), (0, 0), (0, 0)))
    padded_values = jnp.pad(paired[:, :, 1, :], ((pad_rows, 0), (0, 0), (0, 0)))
    padded_ids = jnp.pad(prompt_ids, (pad_rows, 0), constant_values=-1).astype(jnp.int32)
    padded_pos = (jnp.arange(TOKENS + pad_rows, dtype=jnp.int32) - pad_rows).astype(jnp.int32)
    scaler = 1.0 / math.sqrt(HD)

    def one_stretch(stretch_index):
        start = (stretch_index * STRETCH).astype(jnp.int32)
        query_block = lax.dynamic_slice_in_dim(queries, start, STRETCH, 0).reshape(STRETCH, KV_HEADS, GROUP, HD).astype(jnp.float32)
        key_rows = lax.dynamic_slice_in_dim(padded_keys, start, pad_rows + STRETCH, 0).astype(jnp.float32)
        value_rows = lax.dynamic_slice_in_dim(padded_values, start, pad_rows + STRETCH, 0).astype(jnp.float32)
        key_ids = lax.dynamic_slice_in_dim(padded_ids, start, pad_rows + STRETCH, 0)
        key_pos = lax.dynamic_slice_in_dim(padded_pos, start, pad_rows + STRETCH, 0)
        query_ids = lax.dynamic_slice_in_dim(prompt_ids, start, STRETCH, 0)
        query_pos = start + jnp.arange(STRETCH, dtype=jnp.int32)
        scores = jnp.einsum('qhgd,khd->hgqk', query_block, key_rows) * scaler
        allowed = (query_ids[:, None] == key_ids[None, :]) & (key_pos[None, :] <= query_pos[:, None])
        scores = jnp.where(allowed, scores, masked_score)
        row_max = lax.optimization_barrier(jnp.max(scores, axis=-1, keepdims=True))
        probs = jnp.where(allowed, jnp.exp(scores - row_max), 0.0)
        summed = lax.optimization_barrier(jnp.sum(probs, axis=-1))
        probs_low = probs.astype(jnp.bfloat16).astype(jnp.float32)
        weighted = jnp.einsum('hgqk,khd->hgqd', probs_low, value_rows) / summed[..., None]
        return jnp.transpose(weighted, (2, 0, 1, 3)).reshape(STRETCH, Q_HEADS * HD).astype(jnp.bfloat16)
    attention = lax.map(one_stretch, jnp.arange(N_LOOP, dtype=jnp.int32)).reshape(TOKENS, Q_HEADS * HD)
    attention_split = attention.reshape(TOKENS, N_TP, Q_HEADS * HD // N_TP)
    weight_split = out_weight.reshape(N_TP, Q_HEADS * HD // N_TP, D_OUT)

    def add_part(running, tp_index):
        product = jnp.dot(attention_split[:, tp_index, :], weight_split[tp_index], preferred_element_type=jnp.float32)
        product = lax.optimization_barrier(product.astype(jnp.bfloat16)).astype(jnp.float32)
        return (running + product, None)
    running, unused = lax.scan(add_part, jnp.zeros((TOKENS, D_OUT), jnp.float32), jnp.arange(N_TP, dtype=jnp.int32))
    return running.astype(jnp.bfloat16)
```

```python
import functools
import math

import jax
import jax.numpy as jnp
from jax import lax
from jax.experimental import pallas as pl
from jax.experimental.pallas import tpu as pltpu
from jax.sharding import PartitionSpec as P

HD = 128
BLOCKED = -1e30
ROWS = 64
STACK = 2
MESH = pl.DeviceIdType.MESH


def kernel(n_loop, n_tp, reach, q_hbm, kv_hbm, ids_ref, w_hbm, out_ref,
           q_ref, kv_buf, v_buf, id_buf, q_col, bias, attn, w_ref, part, recv_r, recv_l,
           load_sem, kv_send, kv_recv, id_send, id_recv, send_sem, r_sem, l_sem):
    tok = q_ref.shape[0]
    heads = q_ref.shape[1] // HD
    width = part.shape[2]
    blocks = tok // ROWS
    far_last = reach * tok
    scale = math.log2(math.e) / math.sqrt(HD)
    i = lax.axis_index("loop")
    z = lax.axis_index("tp")

    load_q = pltpu.make_async_copy(q_hbm, q_ref, load_sem.at[0])
    load_kv = pltpu.make_async_copy(kv_hbm, kv_buf.at[reach], load_sem.at[1])
    load_w = pltpu.make_async_copy(w_hbm, w_ref, load_sem.at[2])
    load_kv.start()
    load_q.start()
    load_w.start()

    def kv_copy(k):
        return pltpu.make_async_remote_copy(
            src_ref=kv_hbm, dst_ref=kv_buf.at[reach - k], send_sem=kv_send.at[k - 1],
            recv_sem=kv_recv.at[k - 1], device_id=(i + k, z), device_id_type=MESH)

    def id_copy(k):
        return pltpu.make_async_remote_copy(
            src_ref=ids_ref, dst_ref=id_buf.at[reach - k], send_sem=id_send.at[k - 1],
            recv_sem=id_recv.at[k - 1], device_id=(i + k, z), device_id_type=MESH)

    def right_copy(c, b):
        rows = pl.ds(pl.multiple_of(b * ROWS, ROWS), ROWS)
        return pltpu.make_async_remote_copy(
            src_ref=part.at[c, rows], dst_ref=recv_r.at[c, rows], send_sem=send_sem.at[c, b],
            recv_sem=r_sem.at[c, b], device_id=(i, z + 1), device_id_type=MESH)

    def left_copy(c, b):
        rows = pl.ds(pl.multiple_of(b * ROWS, ROWS), ROWS)
        return pltpu.make_async_remote_copy(
            src_ref=part.at[c, rows], dst_ref=recv_l.at[c, rows], send_sem=send_sem.at[c, b],
            recv_sem=l_sem.at[c, b], device_id=(i, z - 1), device_id_type=MESH)

    barrier = pltpu.get_barrier_semaphore()
    for k in range(1, reach + 1):
        @pl.when(i + k < n_loop)
        def _():
            pl.semaphore_signal(barrier, inc=1, device_id=(i + k, z), device_id_type=MESH)

        @pl.when(i - k >= 0)
        def _():
            pl.semaphore_signal(barrier, inc=1, device_id=(i - k, z), device_id_type=MESH)

    @pl.when(z > 0)
    def _():
        pl.semaphore_signal(barrier, inc=1, device_id=(i, z - 1), device_id_type=MESH)

    @pl.when(z < n_tp - 1)
    def _():
        pl.semaphore_signal(barrier, inc=1, device_id=(i, z + 1), device_id_type=MESH)

    greeted = (jnp.minimum(i, reach) + jnp.minimum(n_loop - 1 - i, reach)
               + jnp.minimum(z, 1) + jnp.minimum(n_tp - 1 - z, 1))
    pl.semaphore_wait(barrier, greeted)

    for k in range(1, reach + 1):
        @pl.when(i + k < n_loop)
        def _():
            id_copy(k).start()
            kv_copy(k).start()

    for k in range(1, reach + 1):
        @pl.when(i < k)
        def _():
            kv_buf[reach - k] = jnp.zeros(kv_buf.shape[1:], kv_buf.dtype)
            id_buf[reach - k] = jnp.full(id_buf.shape[1:], -1, id_buf.dtype)
    id_buf[reach] = ids_ref[...]
    own_ids = ids_ref[...].astype(jnp.float32)
    square = (tok, tok)
    q_col[...] = jnp.max(
        jnp.where(lax.broadcasted_iota(jnp.int32, square, 0) == lax.broadcasted_iota(jnp.int32, square, 1),
                  jnp.broadcast_to(own_ids, square), -1.0), axis=1, keepdims=True)
    v_buf[:, HD:] = jnp.ones((v_buf.shape[0], HD), v_buf.dtype)
    load_kv.wait()
    load_q.wait()
    load_w.wait()
    for k in range(1, reach + 1):
        @pl.when(i >= k)
        def _():
            id_copy(k).wait_recv()
            kv_copy(k).wait_recv()
    for s in range(reach + 1):
        v_buf[s * tok:(s + 1) * tok, :HD] = kv_buf[s, :, HD:]

    def compute(b):
        rows = pl.ds(pl.multiple_of(b * ROWS, ROWS), ROWS)
        q_ids = q_col[rows, :]
        shape = (ROWS, tok)
        lower = (lax.broadcasted_iota(jnp.int32, shape, 1)
                 <= lax.broadcasted_iota(jnp.int32, shape, 0) + b * ROWS)
        key_ids = [jnp.broadcast_to(id_buf[s].astype(jnp.float32), shape) for s in range(reach + 1)]
        shared = jnp.where(lower, key_ids[reach], key_ids[0])
        for s, ids in enumerate([shared] + key_ids[1:reach]):
            bias[:, s * tok:(s + 1) * tok] = jnp.where(ids == q_ids, 0.0, BLOCKED)
        keys = kv_buf[:, :, :HD].reshape((reach + 1) * tok, HD)
        for h in range(0, heads, STACK):
            q = jnp.concatenate([q_ref[rows, (h + j) * HD:(h + j + 1) * HD] for j in range(STACK)], axis=0)
            s = lax.dot_general(q, keys, (((1,), (1,)), ((), ())), preferred_element_type=jnp.float32)
            s = s.reshape(STACK, ROWS, (reach + 1) * tok)
            s = jnp.concatenate(
                [jnp.where(lower[None], s[:, :, far_last:], s[:, :, :tok]), s[:, :, tok:far_last]], axis=2)
            s = s * scale + bias[...][None]
            p = jnp.exp2(s - jnp.max(s, axis=2, keepdims=True))
            first = p[:, :, :tok]
            p = jnp.concatenate(
                [jnp.where(lower[None], 0.0, first), p[:, :, tok:], jnp.where(lower[None], first, 0.0)], axis=2)
            p = p.reshape(STACK * ROWS, (reach + 1) * tok).astype(jnp.bfloat16)
            o = jnp.dot(p, v_buf[...], preferred_element_type=jnp.float32)
            o = (o[:, :HD] / o[:, HD:]).astype(jnp.bfloat16)
            for j in range(STACK):
                attn[:, (h + j) * HD:(h + j + 1) * HD] = o[j * ROWS:(j + 1) * ROWS]
        order = []
        for c in range((n_tp + 1) // 2):
            order += [n_tp - 1 - c, c] if c != n_tp - 1 - c else [c]
        for c in order:
            part[c, rows, :] = jnp.dot(
                attn[...], w_ref[:, c * width:(c + 1) * width],
                preferred_element_type=jnp.float32).astype(jnp.bfloat16)
            if c >= 2:
                @pl.when(z == 0)
                def _():
                    right_copy(c, b).start()
            if c < n_tp - 2:
                @pl.when(z == n_tp - 1)
                def _():
                    left_copy(c, b).start()

    def forward_right(b):
        rows = pl.ds(pl.multiple_of(b * ROWS, ROWS), ROWS)
        for c in range(n_tp - 1, 1, -1):
            @pl.when(c > z)
            def _():
                copy = right_copy(c, b)
                copy.wait_recv()
                part[c, rows, :] = (part[c, rows, :].astype(jnp.float32)
                                    + recv_r[c, rows, :].astype(jnp.float32)).astype(jnp.bfloat16)
                copy.start()

    def forward_left(b):
        rows = pl.ds(pl.multiple_of(b * ROWS, ROWS), ROWS)
        for c in range(n_tp - 2):
            @pl.when(c < z)
            def _():
                copy = left_copy(c, b)
                copy.wait_recv()
                part[c, rows, :] = (part[c, rows, :].astype(jnp.float32)
                                    + recv_l[c, rows, :].astype(jnp.float32)).astype(jnp.bfloat16)
                copy.start()

    low_half = z < n_tp // 2
    middle = jnp.logical_and(z > 0, z < n_tp - 1)

    def step(b, carry):
        @pl.when(b < blocks)
        def _():
            compute(b)

        right_b = b - jnp.where(low_half, 1, 2)
        left_b = b - jnp.where(low_half, 2, 1)

        @pl.when(middle & (right_b >= 0) & (right_b < blocks))
        def _():
            forward_right(right_b)

        @pl.when(middle & (left_b >= 0) & (left_b < blocks))
        def _():
            forward_left(left_b)
        return carry

    lax.fori_loop(0, blocks + 2, step, 0)

    @pl.when(z == 0)
    def _():
        for b in range(blocks):
            for c in range(n_tp - 1, 1, -1):
                right_copy(c, b).wait_send()
            if b == blocks - 2:
                for late in range(blocks):
                    right_copy(1, late).start()

    @pl.when(z == n_tp - 1)
    def _():
        for b in range(blocks):
            for c in range(n_tp - 2):
                left_copy(c, b).wait_send()
            if b == blocks - 2:
                for late in range(blocks):
                    left_copy(n_tp - 2, late).start()

    def finish(b, carry):
        rows = pl.ds(pl.multiple_of(b * ROWS, ROWS), ROWS)

        @pl.when(z == 0)
        def _():
            left_copy(z, b).wait_recv()
            out_ref[rows, :] = (part[z, rows, :].astype(jnp.float32)
                                + recv_l[z, rows, :].astype(jnp.float32)).astype(out_ref.dtype)

        @pl.when(z == n_tp - 1)
        def _():
            right_copy(z, b).wait_recv()
            out_ref[rows, :] = (part[z, rows, :].astype(jnp.float32)
                                + recv_r[z, rows, :].astype(jnp.float32)).astype(out_ref.dtype)

        @pl.when(middle)
        def _():
            right_copy(z, b).wait_recv()
            left_copy(z, b).wait_recv()
            out_ref[rows, :] = (part[z, rows, :].astype(jnp.float32)
                                + recv_r[z, rows, :].astype(jnp.float32)
                                + recv_l[z, rows, :].astype(jnp.float32)).astype(out_ref.dtype)
        return carry

    lax.fori_loop(0, blocks, finish, 0)

    for k in range(1, reach + 1):
        @pl.when(i + k < n_loop)
        def _():
            id_copy(k).wait_send()
            kv_copy(k).wait_send()

    def drain(b, carry):
        @pl.when(z == 0)
        def _():
            right_copy(1, b).wait_send()

        @pl.when(z == n_tp - 1)
        def _():
            left_copy(n_tp - 2, b).wait_send()

        for c in range(n_tp):
            @pl.when(middle & (c > z))
            def _():
                right_copy(c, b).wait_send()

            @pl.when(middle & (c < z))
            def _():
                left_copy(c, b).wait_send()
        return carry

    lax.fori_loop(0, blocks, drain, 0)


def per_device(queries, key_values, prompt_ids, out_weight):
    n_loop, n_tp = lax.axis_size("loop"), lax.axis_size("tp")
    tok, q_cols = queries.shape
    depth, d_out = out_weight.shape
    width = d_out // n_tp
    reach = min(8, n_loop // 2)
    blocks = tok // ROWS
    vmem = pltpu.VMEM
    dma = pltpu.SemaphoreType.DMA
    any_spec = pl.BlockSpec(memory_space=pl.ANY)
    vmem_spec = pl.BlockSpec(memory_space=pltpu.VMEM)
    return pl.pallas_call(
        functools.partial(kernel, n_loop, n_tp, reach),
        out_shape=jax.ShapeDtypeStruct((tok, width), jnp.bfloat16),
        in_specs=[any_spec, any_spec, vmem_spec, any_spec],
        out_specs=vmem_spec,
        scratch_shapes=[
            vmem((tok, q_cols), jnp.bfloat16),
            vmem((reach + 1, tok, 2 * HD), jnp.bfloat16),
            vmem(((reach + 1) * tok, 2 * HD), jnp.bfloat16),
            vmem((reach + 1, 1, tok), jnp.int32),
            vmem((tok, 1), jnp.float32),
            vmem((ROWS, reach * tok), jnp.float32),
            vmem((ROWS, q_cols), jnp.bfloat16),
            vmem((depth, d_out), jnp.bfloat16),
            vmem((n_tp, tok, width), jnp.bfloat16),
            vmem((n_tp, tok, width), jnp.bfloat16),
            vmem((n_tp, tok, width), jnp.bfloat16),
            dma((3,)), dma((reach,)), dma((reach,)), dma((reach,)), dma((reach,)),
            dma((n_tp, blocks)), dma((n_tp, blocks)), dma((n_tp, blocks)),
        ],
        compiler_params=pltpu.CompilerParams(
            collective_id=0, has_side_effects=True, vmem_limit_bytes=56 * 1024 * 1024),
        cost_estimate=pl.CostEstimate(flops=3_500_000_000, bytes_accessed=10_000_000, transcendentals=2_000_000),
    )(queries, key_values, prompt_ids.reshape(1, tok), out_weight)


def solution(mesh):
    in_specs = (P("loop", "tp"), P("loop", "tp"), P("loop"), P("tp", None))
    out_specs = P("loop", "tp")
    return jax.shard_map(
        per_device, mesh=mesh, in_specs=in_specs, out_specs=out_specs, check_vma=False
    )
```

```python
import functools
import math

import jax
import jax.numpy as jnp
from jax import lax
from jax.experimental import pallas as pl
from jax.experimental.pallas import tpu as pltpu
from jax.sharding import PartitionSpec as P

HD = 128
BLOCKED = -1e30
ROWS = 64
STACK = 2
MESH = pl.DeviceIdType.MESH


def kernel(n_loop, n_tp, reach, q_hbm, kv_hbm, ids_ref, w_hbm, out_ref, more_ref,
           q_ref, kv_buf, v_buf, id_buf, q_col, bias, attn, w_ref, part, recv_r, recv_l,
           load_sem, kv_send, kv_recv, id_send, id_recv, send_sem, r_sem, l_sem):
    tok = q_ref.shape[0]
    heads = q_ref.shape[1] // HD
    width = part.shape[2]
    blocks = tok // ROWS
    far_last = reach * tok
    scale = math.log2(math.e) / math.sqrt(HD)
    i = lax.axis_index("loop")
    z = lax.axis_index("tp")

    load_q = pltpu.make_async_copy(q_hbm, q_ref, load_sem.at[0])
    load_kv = pltpu.make_async_copy(kv_hbm, kv_buf.at[reach], load_sem.at[1])
    load_w = pltpu.make_async_copy(w_hbm, w_ref, load_sem.at[2])
    load_kv.start()
    load_q.start()
    load_w.start()

    core = lax.rem(i, 2)
    hops = reach // 2

    def chip_copies(d):
        slot = reach - 2 * d
        return [
            pltpu.make_async_remote_copy(
                src_ref=source, dst_ref=target.at[slot], send_sem=sends.at[d - 1],
                recv_sem=arrivals.at[2 * d - 1], device_id=(i + 2 * d, z), device_id_type=MESH)
            for source, target, sends, arrivals in (
                (ids_ref, id_buf, id_send, id_recv), (kv_hbm, kv_buf, kv_send, kv_recv))]

    def up_copies(d):
        return [
            pltpu.make_async_remote_copy(
                src_ref=source if d == 0 else target.at[reach - 2 * d], dst_ref=target.at[reach - 2 * d - 1],
                send_sem=sends.at[hops + d], recv_sem=arrivals.at[2 * d],
                device_id=(i + 1, z), device_id_type=MESH)
            for source, target, sends, arrivals in (
                (ids_ref, id_buf, id_send, id_recv), (kv_hbm, kv_buf, kv_send, kv_recv))]

    def down_copies(d):
        return [
            pltpu.make_async_remote_copy(
                src_ref=target.at[reach - 2 * d], dst_ref=target.at[reach - 2 * d + 1],
                send_sem=sends.at[hops + d - 1], recv_sem=arrivals.at[2 * d - 2],
                device_id=(i - 1, z), device_id_type=MESH)
            for target, sends, arrivals in ((id_buf, id_send, id_recv), (kv_buf, kv_send, kv_recv))]

    def right_copy(c, b):
        rows = pl.ds(pl.multiple_of(b * ROWS, ROWS), ROWS)
        return pltpu.make_async_remote_copy(
            src_ref=part.at[c, rows], dst_ref=recv_r.at[c, rows], send_sem=send_sem.at[c, b],
            recv_sem=r_sem.at[c, b], device_id=(i, z + 1), device_id_type=MESH)

    def left_copy(c, b):
        rows = pl.ds(pl.multiple_of(b * ROWS, ROWS), ROWS)
        return pltpu.make_async_remote_copy(
            src_ref=part.at[c, rows], dst_ref=recv_l.at[c, rows], send_sem=send_sem.at[c, b],
            recv_sem=l_sem.at[c, b], device_id=(i, z - 1), device_id_type=MESH)

    barrier = pltpu.get_barrier_semaphore()
    pl.semaphore_signal(barrier, inc=1, device_id=(i + 1 - 2 * core, z), device_id_type=MESH)
    for d in range(1, hops + 1):
        @pl.when(i + 2 * d < n_loop)
        def _():
            pl.semaphore_signal(barrier, inc=1, device_id=(i + 2 * d, z), device_id_type=MESH)

        @pl.when(i - 2 * d >= 0)
        def _():
            pl.semaphore_signal(barrier, inc=1, device_id=(i - 2 * d, z), device_id_type=MESH)

    @pl.when(z > 0)
    def _():
        pl.semaphore_signal(barrier, inc=1, device_id=(i, z - 1), device_id_type=MESH)

    @pl.when(z < n_tp - 1)
    def _():
        pl.semaphore_signal(barrier, inc=1, device_id=(i, z + 1), device_id_type=MESH)

    chip = i // 2
    greeted = (1 + jnp.minimum(chip, hops) + jnp.minimum(n_loop // 2 - 1 - chip, hops)
               + jnp.minimum(z, 1) + jnp.minimum(n_tp - 1 - z, 1))
    pl.semaphore_wait(barrier, greeted)

    for d in range(1, hops + 1):
        @pl.when(i + 2 * d < n_loop)
        def _():
            for copy in chip_copies(d):
                copy.start()

    @pl.when(core == 0)
    def _():
        for copy in up_copies(0):
            copy.start()

    for k in range(1, reach + 1):
        @pl.when(i < k)
        def _():
            kv_buf[reach - k] = jnp.zeros(kv_buf.shape[1:], kv_buf.dtype)
            id_buf[reach - k] = jnp.full(id_buf.shape[1:], -1, id_buf.dtype)
    id_buf[reach] = ids_ref[...]
    own_ids = ids_ref[...].astype(jnp.float32)
    square = (tok, tok)
    q_col[...] = jnp.max(
        jnp.where(lax.broadcasted_iota(jnp.int32, square, 0) == lax.broadcasted_iota(jnp.int32, square, 1),
                  jnp.broadcast_to(own_ids, square), -1.0), axis=1, keepdims=True)
    v_buf[:, HD:] = jnp.ones((v_buf.shape[0], HD), v_buf.dtype)
    load_kv.wait()
    load_q.wait()
    for d in range(1, hops + 1):
        @pl.when(i >= 2 * d)
        def _():
            for copy in chip_copies(d):
                copy.wait_recv()

            @pl.when(core == 1)
            def _():
                for copy in down_copies(d):
                    copy.start()

            if d < hops:
                @pl.when(core == 0)
                def _():
                    for copy in up_copies(d):
                        copy.start()
    for d in range(1, hops + 1):
        @pl.when((core == 0) & (i >= 2 * d))
        def _():
            for copy in down_copies(d):
                copy.wait_recv()

        @pl.when((core == 1) & (i >= 2 * d - 1))
        def _():
            for copy in up_copies(d - 1):
                copy.wait_recv()
    for s in range(reach + 1):
        v_buf[s * tok:(s + 1) * tok, :HD] = kv_buf[s, :, HD:]

    def compute(b):
        rows = pl.ds(pl.multiple_of(b * ROWS, ROWS), ROWS)
        q_ids = q_col[rows, :]
        shape = (ROWS, tok)
        lower = (lax.broadcasted_iota(jnp.int32, shape, 1)
                 <= lax.broadcasted_iota(jnp.int32, shape, 0) + b * ROWS)
        key_ids = [jnp.broadcast_to(id_buf[s].astype(jnp.float32), shape) for s in range(reach + 1)]
        shared = jnp.where(lower, key_ids[reach], key_ids[0])
        for s, ids in enumerate([shared] + key_ids[1:reach]):
            bias[:, s * tok:(s + 1) * tok] = jnp.where(ids == q_ids, 0.0, BLOCKED)
        keys = kv_buf[:, :, :HD].reshape((reach + 1) * tok, HD)
        for h in range(0, heads, STACK):
            q = jnp.concatenate([q_ref[rows, (h + j) * HD:(h + j + 1) * HD] for j in range(STACK)], axis=0)
            s = lax.dot_general(q, keys, (((1,), (1,)), ((), ())), preferred_element_type=jnp.float32)
            s = s.reshape(STACK, ROWS, (reach + 1) * tok)
            s = jnp.concatenate(
                [jnp.where(lower[None], s[:, :, far_last:], s[:, :, :tok]), s[:, :, tok:far_last]], axis=2)
            s = s * scale + bias[...][None]
            p = jnp.exp2(s - jnp.max(s, axis=2, keepdims=True))
            first = p[:, :, :tok]
            p = jnp.concatenate(
                [jnp.where(lower[None], 0.0, first), p[:, :, tok:], jnp.where(lower[None], first, 0.0)], axis=2)
            p = p.reshape(STACK * ROWS, (reach + 1) * tok).astype(jnp.bfloat16)
            o = jnp.dot(p, v_buf[...], preferred_element_type=jnp.float32)
            o = (o[:, :HD] / o[:, HD:]).astype(jnp.bfloat16)
            for j in range(STACK):
                attn[:, (h + j) * HD:(h + j + 1) * HD] = o[j * ROWS:(j + 1) * ROWS]

        @pl.when(b == 0)
        def _():
            load_w.wait()
        order = []
        for c in range((n_tp + 1) // 2):
            order += [n_tp - 1 - c, c] if c != n_tp - 1 - c else [c]
        for c in order:
            part[c, rows, :] = jnp.dot(
                attn[...], w_ref[:, c * width:(c + 1) * width],
                preferred_element_type=jnp.float32).astype(jnp.bfloat16)
            if c >= 2:
                @pl.when(z == 0)
                def _():
                    right_copy(c, b).start()
            if c < n_tp - 2:
                @pl.when(z == n_tp - 1)
                def _():
                    left_copy(c, b).start()

    def forward_right(b):
        rows = pl.ds(pl.multiple_of(b * ROWS, ROWS), ROWS)
        for c in range(n_tp - 1, 1, -1):
            @pl.when(c > z)
            def _():
                copy = right_copy(c, b)
                copy.wait_recv()
                part[c, rows, :] = (part[c, rows, :].astype(jnp.float32)
                                    + recv_r[c, rows, :].astype(jnp.float32)).astype(jnp.bfloat16)
                copy.start()

    def forward_left(b):
        rows = pl.ds(pl.multiple_of(b * ROWS, ROWS), ROWS)
        for c in range(n_tp - 2):
            @pl.when(c < z)
            def _():
                copy = left_copy(c, b)
                copy.wait_recv()
                part[c, rows, :] = (part[c, rows, :].astype(jnp.float32)
                                    + recv_l[c, rows, :].astype(jnp.float32)).astype(jnp.bfloat16)
                copy.start()

    low_half = z < n_tp // 2
    middle = jnp.logical_and(z > 0, z < n_tp - 1)

    def step(b, carry):
        @pl.when(b < blocks)
        def _():
            compute(b)

        right_b = b - jnp.where(low_half, 1, 2)
        left_b = b - jnp.where(low_half, 2, 1)

        @pl.when(middle & (right_b >= 0) & (right_b < blocks))
        def _():
            forward_right(right_b)

        @pl.when(middle & (left_b >= 0) & (left_b < blocks))
        def _():
            forward_left(left_b)
        return carry

    lax.fori_loop(0, blocks + 2, step, 0)

    @pl.when(z == 0)
    def _():
        for b in range(blocks):
            for c in range(n_tp - 1, 1, -1):
                right_copy(c, b).wait_send()
            if b == blocks - 2:
                for late in range(blocks):
                    right_copy(1, late).start()

    @pl.when(z == n_tp - 1)
    def _():
        for b in range(blocks):
            for c in range(n_tp - 2):
                left_copy(c, b).wait_send()
            if b == blocks - 2:
                for late in range(blocks):
                    left_copy(n_tp - 2, late).start()

    def finish(b, carry):
        rows = pl.ds(pl.multiple_of(b * ROWS, ROWS), ROWS)

        @pl.when(z == 0)
        def _():
            left_copy(z, b).wait_recv()
            out_ref[rows, :] = part[z, rows, :]
            more_ref[rows, :] = recv_l[z, rows, :]

        @pl.when(z == n_tp - 1)
        def _():
            right_copy(z, b).wait_recv()
            out_ref[rows, :] = part[z, rows, :]
            more_ref[rows, :] = recv_r[z, rows, :]

        @pl.when(middle)
        def _():
            right_copy(z, b).wait_recv()
            left_copy(z, b).wait_recv()
            out_ref[rows, :] = part[z, rows, :]
            more_ref[rows, :] = (recv_r[z, rows, :].astype(jnp.float32)
                                 + recv_l[z, rows, :].astype(jnp.float32)).astype(out_ref.dtype)
        return carry

    lax.fori_loop(0, blocks, finish, 0)

    for d in range(1, hops + 1):
        @pl.when(i + 2 * d < n_loop)
        def _():
            for copy in chip_copies(d):
                copy.wait_send()

        @pl.when((core == 1) & (i >= 2 * d))
        def _():
            for copy in down_copies(d):
                copy.wait_send()

        @pl.when((core == 0) & (i >= 2 * d - 2))
        def _():
            for copy in up_copies(d - 1):
                copy.wait_send()

    def drain(b, carry):
        @pl.when(z == 0)
        def _():
            right_copy(1, b).wait_send()

        @pl.when(z == n_tp - 1)
        def _():
            left_copy(n_tp - 2, b).wait_send()

        for c in range(n_tp):
            @pl.when(middle & (c > z))
            def _():
                right_copy(c, b).wait_send()

            @pl.when(middle & (c < z))
            def _():
                left_copy(c, b).wait_send()
        return carry

    lax.fori_loop(0, blocks, drain, 0)


def per_device(queries, key_values, prompt_ids, out_weight):
    n_loop, n_tp = lax.axis_size("loop"), lax.axis_size("tp")
    tok, q_cols = queries.shape
    depth, d_out = out_weight.shape
    width = d_out // n_tp
    reach = min(8, n_loop // 2)
    blocks = tok // ROWS
    vmem = pltpu.VMEM
    dma = pltpu.SemaphoreType.DMA
    any_spec = pl.BlockSpec(memory_space=pl.ANY)
    vmem_spec = pl.BlockSpec(memory_space=pltpu.VMEM)
    one, more = pl.pallas_call(
        functools.partial(kernel, n_loop, n_tp, reach),
        out_shape=[jax.ShapeDtypeStruct((tok, width), jnp.bfloat16)] * 2,
        in_specs=[any_spec, any_spec, vmem_spec, any_spec],
        out_specs=[vmem_spec] * 2,
        scratch_shapes=[
            vmem((tok, q_cols), jnp.bfloat16),
            vmem((reach + 1, tok, 2 * HD), jnp.bfloat16),
            vmem(((reach + 1) * tok, 2 * HD), jnp.bfloat16),
            vmem((reach + 1, 1, tok), jnp.int32),
            vmem((tok, 1), jnp.float32),
            vmem((ROWS, reach * tok), jnp.float32),
            vmem((ROWS, q_cols), jnp.bfloat16),
            vmem((depth, d_out), jnp.bfloat16),
            vmem((n_tp, tok, width), jnp.bfloat16),
            vmem((n_tp, tok, width), jnp.bfloat16),
            vmem((n_tp, tok, width), jnp.bfloat16),
            dma((3,)), dma((reach,)), dma((reach,)), dma((reach,)), dma((reach,)),
            dma((n_tp, blocks)), dma((n_tp, blocks)), dma((n_tp, blocks)),
        ],
        compiler_params=pltpu.CompilerParams(
            collective_id=0, has_side_effects=True, vmem_limit_bytes=56 * 1024 * 1024),
        cost_estimate=pl.CostEstimate(flops=3_500_000_000, bytes_accessed=10_000_000, transcendentals=2_000_000),
    )(queries, key_values, prompt_ids.reshape(1, tok), out_weight)
    return (one.astype(jnp.float32) + more.astype(jnp.float32)).astype(jnp.bfloat16)


def solution(mesh):
    in_specs = (P("loop", "tp"), P("loop", "tp"), P("loop"), P("tp", None))
    out_specs = P("loop", "tp")
    return jax.shard_map(
        per_device, mesh=mesh, in_specs=in_specs, out_specs=out_specs, check_vma=False
    )
```

```python
import functools
import math

import jax
import jax.numpy as jnp
from jax import lax
from jax.experimental import pallas as pl
from jax.experimental.pallas import tpu as pltpu
from jax.sharding import PartitionSpec as P

HD = 128
BLOCKED = -1e30
ROWS = 32
STACK = 4
MESH = pl.DeviceIdType.MESH


def kernel(n_loop, n_tp, reach, q_hbm, kv_hbm, ids_hbm, w_hbm, out_ref,
           q_ref, kv_buf, v_buf, id_buf, q_col, bias, attn, w_ref, part, recv_r, recv_l,
           load_sem, kv_send, kv_recv, id_send, id_recv, send_sem, r_sem, l_sem):
    tok = q_ref.shape[0]
    heads = q_ref.shape[1] // HD
    width = part.shape[2]
    blocks = tok // ROWS
    far_last = reach * tok
    scale = math.log2(math.e) / math.sqrt(HD)
    i = lax.axis_index("loop")
    z = lax.axis_index("tp")

    load_q = pltpu.make_async_copy(q_hbm, q_ref, load_sem.at[0])
    load_kv = pltpu.make_async_copy(kv_hbm, kv_buf.at[reach], load_sem.at[1])
    load_w = pltpu.make_async_copy(w_hbm, w_ref, load_sem.at[2])
    load_ids = pltpu.make_async_copy(ids_hbm, id_buf.at[reach], load_sem.at[3])
    load_ids.start()
    load_kv.start()
    load_q.start()
    load_w.start()

    core = lax.rem(i, 2)
    hops = reach // 2

    def chip_copies(d):
        slot = reach - 2 * d
        return [
            pltpu.make_async_remote_copy(
                src_ref=source, dst_ref=target.at[slot], send_sem=sends.at[d - 1],
                recv_sem=arrivals.at[2 * d - 1], device_id=(i + 2 * d, z), device_id_type=MESH)
            for source, target, sends, arrivals in (
                (ids_hbm, id_buf, id_send, id_recv), (kv_hbm, kv_buf, kv_send, kv_recv))]

    def up_copies(d):
        return [
            pltpu.make_async_remote_copy(
                src_ref=source if d == 0 else target.at[reach - 2 * d], dst_ref=target.at[reach - 2 * d - 1],
                send_sem=sends.at[hops + d], recv_sem=arrivals.at[2 * d],
                device_id=(i + 1, z), device_id_type=MESH)
            for source, target, sends, arrivals in (
                (ids_hbm, id_buf, id_send, id_recv), (kv_hbm, kv_buf, kv_send, kv_recv))]

    def down_copies(d):
        return [
            pltpu.make_async_remote_copy(
                src_ref=target.at[reach - 2 * d], dst_ref=target.at[reach - 2 * d + 1],
                send_sem=sends.at[hops + d - 1], recv_sem=arrivals.at[2 * d - 2],
                device_id=(i - 1, z), device_id_type=MESH)
            for target, sends, arrivals in ((id_buf, id_send, id_recv), (kv_buf, kv_send, kv_recv))]

    def right_copy(c, b):
        rows = pl.ds(pl.multiple_of(b * ROWS, ROWS), ROWS)
        return pltpu.make_async_remote_copy(
            src_ref=part.at[c, rows], dst_ref=recv_r.at[c, rows], send_sem=send_sem.at[c, b],
            recv_sem=r_sem.at[c, b], device_id=(i, z + 1), device_id_type=MESH)

    def left_copy(c, b):
        rows = pl.ds(pl.multiple_of(b * ROWS, ROWS), ROWS)
        return pltpu.make_async_remote_copy(
            src_ref=part.at[c, rows], dst_ref=recv_l.at[c, rows], send_sem=send_sem.at[c, b],
            recv_sem=l_sem.at[c, b], device_id=(i, z - 1), device_id_type=MESH)

    barrier = pltpu.get_barrier_semaphore()
    pl.semaphore_signal(barrier, inc=1, device_id=(i + 1 - 2 * core, z), device_id_type=MESH)
    for d in range(1, hops + 1):
        @pl.when(i + 2 * d < n_loop)
        def _():
            pl.semaphore_signal(barrier, inc=1, device_id=(i + 2 * d, z), device_id_type=MESH)

        @pl.when(i - 2 * d >= 0)
        def _():
            pl.semaphore_signal(barrier, inc=1, device_id=(i - 2 * d, z), device_id_type=MESH)

    @pl.when(z > 0)
    def _():
        pl.semaphore_signal(barrier, inc=1, device_id=(i, z - 1), device_id_type=MESH)

    @pl.when(z < n_tp - 1)
    def _():
        pl.semaphore_signal(barrier, inc=1, device_id=(i, z + 1), device_id_type=MESH)

    chip = i // 2
    greeted = (1 + jnp.minimum(chip, hops) + jnp.minimum(n_loop // 2 - 1 - chip, hops)
               + jnp.minimum(z, 1) + jnp.minimum(n_tp - 1 - z, 1))
    pl.semaphore_wait(barrier, greeted)

    for d in range(1, hops + 1):
        @pl.when(i + 2 * d < n_loop)
        def _():
            for copy in chip_copies(d):
                copy.start()

    @pl.when(core == 0)
    def _():
        for copy in up_copies(0):
            copy.start()

    for k in range(1, reach + 1):
        @pl.when(i < k)
        def _():
            kv_buf[reach - k] = jnp.zeros(kv_buf.shape[1:], kv_buf.dtype)
            id_buf[reach - k] = jnp.full(id_buf.shape[1:], -1, id_buf.dtype)
    load_ids.wait()
    own_ids = id_buf[reach].astype(jnp.float32)
    square = (tok, tok)
    q_col[...] = jnp.max(
        jnp.where(lax.broadcasted_iota(jnp.int32, square, 0) == lax.broadcasted_iota(jnp.int32, square, 1),
                  jnp.broadcast_to(own_ids, square), -1.0), axis=1, keepdims=True)
    v_buf[:, HD:] = jnp.ones((v_buf.shape[0], HD), v_buf.dtype)
    load_kv.wait()
    load_q.wait()
    for d in range(1, hops + 1):
        @pl.when(i >= 2 * d)
        def _():
            for copy in chip_copies(d):
                copy.wait_recv()

            @pl.when(core == 1)
            def _():
                for copy in down_copies(d):
                    copy.start()

            if d < hops:
                @pl.when(core == 0)
                def _():
                    for copy in up_copies(d):
                        copy.start()
    for d in range(1, hops + 1):
        @pl.when((core == 0) & (i >= 2 * d))
        def _():
            for copy in down_copies(d):
                copy.wait_recv()

        @pl.when((core == 1) & (i >= 2 * d - 1))
        def _():
            for copy in up_copies(d - 1):
                copy.wait_recv()
    for s in range(reach + 1):
        v_buf[s * tok:(s + 1) * tok, :HD] = kv_buf[s, :, HD:]

    def compute(b):
        rows = pl.ds(pl.multiple_of(b * ROWS, ROWS), ROWS)
        q_ids = q_col[rows, :]
        shape = (ROWS, tok)
        lower = (lax.broadcasted_iota(jnp.int32, shape, 1)
                 <= lax.broadcasted_iota(jnp.int32, shape, 0) + b * ROWS)
        key_ids = [jnp.broadcast_to(id_buf[s].astype(jnp.float32), shape) for s in range(reach + 1)]
        shared = jnp.where(lower, key_ids[reach], key_ids[0])
        for s, ids in enumerate([shared] + key_ids[1:reach]):
            bias[:, s * tok:(s + 1) * tok] = jnp.where(ids == q_ids, 0.0, BLOCKED)
        keys = kv_buf[:, :, :HD].reshape((reach + 1) * tok, HD)
        for h in range(0, heads, STACK):
            q = jnp.concatenate([q_ref[rows, (h + j) * HD:(h + j + 1) * HD] for j in range(STACK)], axis=0)
            s = lax.dot_general(q, keys, (((1,), (1,)), ((), ())), preferred_element_type=jnp.float32)
            s = s.reshape(STACK, ROWS, (reach + 1) * tok)
            s = jnp.concatenate(
                [jnp.where(lower[None], s[:, :, far_last:], s[:, :, :tok]), s[:, :, tok:far_last]], axis=2)
            s = s * scale + bias[...][None]
            p = jnp.exp2(s - jnp.max(s, axis=2, keepdims=True))
            first = p[:, :, :tok]
            p = jnp.concatenate(
                [jnp.where(lower[None], 0.0, first), p[:, :, tok:], jnp.where(lower[None], first, 0.0)], axis=2)
            p = p.reshape(STACK * ROWS, (reach + 1) * tok).astype(jnp.bfloat16)
            o = jnp.dot(p, v_buf[...], preferred_element_type=jnp.float32)
            o = (o[:, :HD] / o[:, HD:]).astype(jnp.bfloat16)
            for j in range(STACK):
                attn[:, (h + j) * HD:(h + j + 1) * HD] = o[j * ROWS:(j + 1) * ROWS]

        @pl.when(b == 0)
        def _():
            load_w.wait()
        order = []
        for c in range((n_tp + 1) // 2):
            order += [n_tp - 1 - c, c] if c != n_tp - 1 - c else [c]
        for c in order:
            part[c, rows, :] = jnp.dot(
                attn[...], w_ref[:, c * width:(c + 1) * width],
                preferred_element_type=jnp.float32).astype(jnp.bfloat16)
            if c >= 2:
                @pl.when(z == 0)
                def _():
                    right_copy(c, b).start()
            if c < n_tp - 2:
                @pl.when(z == n_tp - 1)
                def _():
                    left_copy(c, b).start()

    def forward_right(b):
        rows = pl.ds(pl.multiple_of(b * ROWS, ROWS), ROWS)
        for c in range(n_tp - 1, 1, -1):
            @pl.when(c > z)
            def _():
                copy = right_copy(c, b)
                copy.wait_recv()
                part[c, rows, :] = (part[c, rows, :].astype(jnp.float32)
                                    + recv_r[c, rows, :].astype(jnp.float32)).astype(jnp.bfloat16)
                copy.start()

    def forward_left(b):
        rows = pl.ds(pl.multiple_of(b * ROWS, ROWS), ROWS)
        for c in range(n_tp - 2):
            @pl.when(c < z)
            def _():
                copy = left_copy(c, b)
                copy.wait_recv()
                part[c, rows, :] = (part[c, rows, :].astype(jnp.float32)
                                    + recv_l[c, rows, :].astype(jnp.float32)).astype(jnp.bfloat16)
                copy.start()

    low_half = z < n_tp // 2
    middle = jnp.logical_and(z > 0, z < n_tp - 1)

    def step(b, carry):
        @pl.when(b < blocks)
        def _():
            compute(b)

        right_b = b - jnp.where(low_half, 1, 2)
        left_b = b - jnp.where(low_half, 2, 1)

        @pl.when(middle & low_half & (right_b >= 0) & (right_b < blocks))
        def _():
            forward_right(right_b)

        @pl.when(middle & (left_b >= 0) & (left_b < blocks))
        def _():
            forward_left(left_b)

        @pl.when(middle & jnp.logical_not(low_half) & (right_b >= 0) & (right_b < blocks))
        def _():
            forward_right(right_b)
        return carry

    lax.fori_loop(0, blocks + 2, step, 0)

    @pl.when(z == 0)
    def _():
        for b in range(blocks):
            for c in range(n_tp - 1, 1, -1):
                right_copy(c, b).wait_send()
            if b == blocks - 2:
                for late in range(blocks):
                    right_copy(1, late).start()

    @pl.when(z == n_tp - 1)
    def _():
        for b in range(blocks):
            for c in range(n_tp - 2):
                left_copy(c, b).wait_send()
            if b == blocks - 2:
                for late in range(blocks):
                    left_copy(n_tp - 2, late).start()

    def finish(b, carry):
        rows = pl.ds(pl.multiple_of(b * ROWS, ROWS), ROWS)

        @pl.when(z == 0)
        def _():
            left_copy(z, b).wait_recv()
            out_ref[rows, :] = (part[z, rows, :].astype(jnp.float32)
                                + recv_l[z, rows, :].astype(jnp.float32)).astype(out_ref.dtype)

        @pl.when(z == n_tp - 1)
        def _():
            right_copy(z, b).wait_recv()
            out_ref[rows, :] = (part[z, rows, :].astype(jnp.float32)
                                + recv_r[z, rows, :].astype(jnp.float32)).astype(out_ref.dtype)

        @pl.when(middle)
        def _():
            right_copy(z, b).wait_recv()
            left_copy(z, b).wait_recv()
            out_ref[rows, :] = (part[z, rows, :].astype(jnp.float32)
                                + recv_r[z, rows, :].astype(jnp.float32)
                                + recv_l[z, rows, :].astype(jnp.float32)).astype(out_ref.dtype)
        return carry

    lax.fori_loop(0, blocks, finish, 0)

    for d in range(1, hops + 1):
        @pl.when(i + 2 * d < n_loop)
        def _():
            for copy in chip_copies(d):
                copy.wait_send()

        @pl.when((core == 1) & (i >= 2 * d))
        def _():
            for copy in down_copies(d):
                copy.wait_send()

        @pl.when((core == 0) & (i >= 2 * d - 2))
        def _():
            for copy in up_copies(d - 1):
                copy.wait_send()

    def drain(b, carry):
        @pl.when(z == 0)
        def _():
            right_copy(1, b).wait_send()

        @pl.when(z == n_tp - 1)
        def _():
            left_copy(n_tp - 2, b).wait_send()

        for c in range(n_tp):
            @pl.when(middle & (c > z))
            def _():
                right_copy(c, b).wait_send()

            @pl.when(middle & (c < z))
            def _():
                left_copy(c, b).wait_send()
        return carry

    lax.fori_loop(0, blocks, drain, 0)


def per_device(queries, key_values, prompt_ids, out_weight):
    n_loop, n_tp = lax.axis_size("loop"), lax.axis_size("tp")
    tok, q_cols = queries.shape
    depth, d_out = out_weight.shape
    width = d_out // n_tp
    reach = min(8, n_loop // 2)
    blocks = tok // ROWS
    vmem = pltpu.VMEM
    dma = pltpu.SemaphoreType.DMA
    any_spec = pl.BlockSpec(memory_space=pl.ANY)
    vmem_spec = pl.BlockSpec(memory_space=pltpu.VMEM)
    return pl.pallas_call(
        functools.partial(kernel, n_loop, n_tp, reach),
        out_shape=pltpu.VMEM((tok, width), jnp.bfloat16),
        in_specs=[any_spec] * 4,
        out_specs=vmem_spec,
        scratch_shapes=[
            vmem((tok, q_cols), jnp.bfloat16),
            vmem((reach + 1, tok, 2 * HD), jnp.bfloat16),
            vmem(((reach + 1) * tok, 2 * HD), jnp.bfloat16),
            vmem((reach + 1, 1, tok), jnp.int32),
            vmem((tok, 1), jnp.float32),
            vmem((ROWS, reach * tok), jnp.float32),
            vmem((ROWS, q_cols), jnp.bfloat16),
            vmem((depth, d_out), jnp.bfloat16),
            vmem((n_tp, tok, width), jnp.bfloat16),
            vmem((n_tp, tok, width), jnp.bfloat16),
            vmem((n_tp, tok, width), jnp.bfloat16),
            dma((4,)), dma((reach,)), dma((reach,)), dma((reach,)), dma((reach,)),
            dma((n_tp, blocks)), dma((n_tp, blocks)), dma((n_tp, blocks)),
        ],
        compiler_params=pltpu.CompilerParams(
            collective_id=0, has_side_effects=True, vmem_limit_bytes=32 * 1024 * 1024),
        cost_estimate=pl.CostEstimate(flops=3_500_000_000, bytes_accessed=10_000_000, transcendentals=2_000_000),
    )(*(pltpu.with_memory_space_constraint(x, pltpu.HBM)
        for x in (queries, key_values, prompt_ids.reshape(1, tok), out_weight)))


def solution(mesh):
    in_specs = (P("loop", "tp"), P("loop", "tp"), P("loop"), P("tp", None))
    out_specs = P("loop", "tp")
    return jax.shard_map(
        per_device, mesh=mesh, in_specs=in_specs, out_specs=out_specs, check_vma=False
    )
```

```python
import functools
import math

import jax
import jax.numpy as jnp
from jax import lax
from jax.experimental import pallas as pl
from jax.experimental.pallas import tpu as pltpu
from jax.sharding import PartitionSpec as P

HD = 128
BLOCKED = -1e30
ROWS = 32
STACK = 4
MESH = pl.DeviceIdType.MESH


def kernel(n_loop, n_tp, reach, q_hbm, kv_hbm, ids_hbm, w_hbm, out_ref,
           q_ref, kv_buf, v_buf, id_buf, q_col, bias, probs, attn, w_ref, part, recv_r, recv_l,
           load_sem, kv_send, kv_recv, relay_send, pair_send, pair_recv, id_send, id_recv, send_sem, r_sem, l_sem):
    tok = q_ref.shape[0]
    heads = q_ref.shape[1] // HD
    width = part.shape[2]
    blocks = tok // ROWS
    far_last = reach * tok
    scale = math.log2(math.e) / math.sqrt(HD)
    i = lax.axis_index("loop")
    z = lax.axis_index("tp")

    load_q = pltpu.make_async_copy(q_hbm, q_ref, load_sem.at[0])
    load_kv = pltpu.make_async_copy(kv_hbm, kv_buf.at[reach], load_sem.at[1])
    load_w = pltpu.make_async_copy(w_hbm, w_ref, load_sem.at[2])
    load_ids = pltpu.make_async_copy(ids_hbm, id_buf.at[reach], load_sem.at[3])
    load_ids.start()
    load_kv.start()
    load_q.start()
    load_w.start()

    core = lax.rem(i, 2)
    chip = i // 2
    hops = reach // 2

    half = tok // 2
    relay = n_loop == 8 and hops == 2

    def id_chip(d):
        return pltpu.make_async_remote_copy(
            src_ref=ids_hbm, dst_ref=id_buf.at[reach - 2 * d], send_sem=id_send.at[d - 1],
            recv_sem=id_recv.at[2 * d - 1], device_id=(i + 2 * d, z), device_id_type=MESH)

    def id_up(d):
        return pltpu.make_async_remote_copy(
            src_ref=ids_hbm if d == 0 else id_buf.at[reach - 2 * d], dst_ref=id_buf.at[reach - 2 * d - 1],
            send_sem=id_send.at[hops + d], recv_sem=id_recv.at[2 * d],
            device_id=(i + 1, z), device_id_type=MESH)

    def id_down(d):
        return pltpu.make_async_remote_copy(
            src_ref=id_buf.at[reach - 2 * d], dst_ref=id_buf.at[reach - 2 * d + 1],
            send_sem=id_send.at[hops + d - 1], recv_sem=id_recv.at[2 * d - 2],
            device_id=(i - 1, z), device_id_type=MESH)

    def chip_copy(t, h, d):
        rows, cols = pl.ds(h * half, half), pl.ds(t * HD, HD)
        return pltpu.make_async_remote_copy(
            src_ref=kv_hbm.at[rows, cols], dst_ref=kv_buf.at[reach - 2 * d, rows, cols],
            send_sem=kv_send.at[t, h, d - 1], recv_sem=kv_recv.at[t, h, d - 1],
            device_id=(i + 2 * d, z), device_id_type=MESH)

    def relay_copy(t):
        rows, cols = pl.ds(0, half), pl.ds(t * HD, HD)
        return pltpu.make_async_remote_copy(
            src_ref=kv_buf.at[reach - 4, rows, cols], dst_ref=kv_buf.at[reach - 2, rows, cols],
            send_sem=relay_send.at[t], recv_sem=kv_recv.at[t, 0, 0],
            device_id=(i - 2, z), device_id_type=MESH)

    def up_copy(t, d):
        cols = pl.ds(t * HD, HD)
        return pltpu.make_async_remote_copy(
            src_ref=kv_hbm.at[:, cols] if d == 0 else kv_buf.at[reach - 2 * d, :, cols],
            dst_ref=kv_buf.at[reach - 2 * d - 1, :, cols],
            send_sem=pair_send.at[t, d], recv_sem=pair_recv.at[t, d],
            device_id=(i + 1, z), device_id_type=MESH)

    def down_copy(t, d):
        cols = pl.ds(t * HD, HD)
        return pltpu.make_async_remote_copy(
            src_ref=kv_buf.at[reach - 2 * d, :, cols], dst_ref=kv_buf.at[reach - 2 * d + 1, :, cols],
            send_sem=pair_send.at[t, d - 1], recv_sem=pair_recv.at[t, d - 1],
            device_id=(i - 1, z), device_id_type=MESH)

    def chip_each(t, act):
        for h in range(2):
            for d in range(hops, 0, -1):
                there = i + 2 * d < n_loop
                if relay and h == 0 and d == 1:
                    there = there & (chip != 1)

                @pl.when(there)
                def _():
                    act(chip_copy(t, h, d))

    def collect(t):
        for d in range(hops, 0, -1):
            @pl.when(i >= 2 * d)
            def _():
                chip_copy(t, 0, d).wait_recv()
                if relay and d == 2:
                    @pl.when(chip == 3)
                    def _():
                        relay_copy(t).start()
                chip_copy(t, 1, d).wait_recv()

                @pl.when(core == 1)
                def _():
                    down_copy(t, d).start()

                if d < hops:
                    @pl.when(core == 0)
                    def _():
                        up_copy(t, d).start()
        for d in range(1, hops + 1):
            @pl.when((core == 0) & (i >= 2 * d))
            def _():
                down_copy(t, d).wait_recv()

            @pl.when((core == 1) & (i >= 2 * d - 1))
            def _():
                up_copy(t, d - 1).wait_recv()

    def right_copy(c, b):
        rows = pl.ds(pl.multiple_of(b * ROWS, ROWS), ROWS)
        return pltpu.make_async_remote_copy(
            src_ref=part.at[c, rows], dst_ref=recv_r.at[c, rows], send_sem=send_sem.at[c, b],
            recv_sem=r_sem.at[c, b], device_id=(i, z + 1), device_id_type=MESH)

    def left_copy(c, b):
        rows = pl.ds(pl.multiple_of(b * ROWS, ROWS), ROWS)
        return pltpu.make_async_remote_copy(
            src_ref=part.at[c, rows], dst_ref=recv_l.at[c, rows], send_sem=send_sem.at[c, b],
            recv_sem=l_sem.at[c, b], device_id=(i, z - 1), device_id_type=MESH)

    barrier = pltpu.get_barrier_semaphore()
    pl.semaphore_signal(barrier, inc=1, device_id=(i + 1 - 2 * core, z), device_id_type=MESH)
    for d in range(1, hops + 1):
        @pl.when(i + 2 * d < n_loop)
        def _():
            pl.semaphore_signal(barrier, inc=1, device_id=(i + 2 * d, z), device_id_type=MESH)

        @pl.when(i - 2 * d >= 0)
        def _():
            pl.semaphore_signal(barrier, inc=1, device_id=(i - 2 * d, z), device_id_type=MESH)

    @pl.when(z > 0)
    def _():
        pl.semaphore_signal(barrier, inc=1, device_id=(i, z - 1), device_id_type=MESH)

    @pl.when(z < n_tp - 1)
    def _():
        pl.semaphore_signal(barrier, inc=1, device_id=(i, z + 1), device_id_type=MESH)

    greeted = (1 + jnp.minimum(chip, hops) + jnp.minimum(n_loop // 2 - 1 - chip, hops)
               + jnp.minimum(z, 1) + jnp.minimum(n_tp - 1 - z, 1))
    pl.semaphore_wait(barrier, greeted)

    for d in range(1, hops + 1):
        @pl.when(i + 2 * d < n_loop)
        def _():
            id_chip(d).start()

    chip_each(0, lambda copy: copy.start())

    @pl.when(core == 0)
    def _():
        id_up(0).start()
        up_copy(0, 0).start()

    for k in range(1, reach + 1):
        @pl.when(i < k)
        def _():
            kv_buf[reach - k] = jnp.zeros(kv_buf.shape[1:], kv_buf.dtype)
            id_buf[reach - k] = jnp.full(id_buf.shape[1:], -1, id_buf.dtype)
    load_ids.wait()
    own_ids = id_buf[reach].astype(jnp.float32)
    square = (tok, tok)
    q_col[...] = jnp.max(
        jnp.where(lax.broadcasted_iota(jnp.int32, square, 0) == lax.broadcasted_iota(jnp.int32, square, 1),
                  jnp.broadcast_to(own_ids, square), -1.0), axis=1, keepdims=True)
    v_buf[:, HD:] = jnp.ones((v_buf.shape[0], HD), v_buf.dtype)
    load_kv.wait()
    load_q.wait()

    chip_each(0, lambda copy: copy.wait_send())
    chip_each(1, lambda copy: copy.start())

    @pl.when(core == 0)
    def _():
        up_copy(1, 0).start()

    for d in range(1, hops + 1):
        @pl.when(i >= 2 * d)
        def _():
            id_chip(d).wait_recv()

            @pl.when(core == 1)
            def _():
                id_down(d).start()

            if d < hops:
                @pl.when(core == 0)
                def _():
                    id_up(d).start()
    collect(0)
    for d in range(1, hops + 1):
        @pl.when((core == 0) & (i >= 2 * d))
        def _():
            id_down(d).wait_recv()

        @pl.when((core == 1) & (i >= 2 * d - 1))
        def _():
            id_up(d - 1).wait_recv()

    def compute(b):
        rows = pl.ds(pl.multiple_of(b * ROWS, ROWS), ROWS)
        q_ids = q_col[rows, :]
        shape = (ROWS, tok)
        lower = (lax.broadcasted_iota(jnp.int32, shape, 1)
                 <= lax.broadcasted_iota(jnp.int32, shape, 0) + b * ROWS)
        key_ids = [jnp.broadcast_to(id_buf[s].astype(jnp.float32), shape) for s in range(reach + 1)]
        shared = jnp.where(lower, key_ids[reach], key_ids[0])
        for s, ids in enumerate([shared] + key_ids[1:reach]):
            bias[:, s * tok:(s + 1) * tok] = jnp.where(ids == q_ids, 0.0, BLOCKED)
        keys = kv_buf[:, :, :HD].reshape((reach + 1) * tok, HD)
        for h in range(0, heads, STACK):
            q = jnp.concatenate([q_ref[rows, (h + j) * HD:(h + j + 1) * HD] for j in range(STACK)], axis=0)
            s = lax.dot_general(q, keys, (((1,), (1,)), ((), ())), preferred_element_type=jnp.float32)
            s = s.reshape(STACK, ROWS, (reach + 1) * tok)
            s = jnp.concatenate(
                [jnp.where(lower[None], s[:, :, far_last:], s[:, :, :tok]), s[:, :, tok:far_last]], axis=2)
            s = s * scale + bias[...][None]
            p = jnp.exp2(s - jnp.max(s, axis=2, keepdims=True))
            first = p[:, :, :tok]
            p = jnp.concatenate(
                [jnp.where(lower[None], 0.0, first), p[:, :, tok:], jnp.where(lower[None], first, 0.0)], axis=2)
            probs[h * ROWS:(h + STACK) * ROWS, :] = p.reshape(STACK * ROWS, (reach + 1) * tok).astype(jnp.bfloat16)

        @pl.when(b == 0)
        def _():
            collect(1)
            for s in range(reach + 1):
                v_buf[s * tok:(s + 1) * tok, :HD] = kv_buf[s, :, HD:]

        o = jnp.dot(probs[...], v_buf[...], preferred_element_type=jnp.float32)
        o = (o[:, :HD] / o[:, HD:]).astype(jnp.bfloat16)
        for h in range(heads):
            attn[:, h * HD:(h + 1) * HD] = o[h * ROWS:(h + 1) * ROWS]

        @pl.when(b == 0)
        def _():
            load_w.wait()
        order = []
        for c in range((n_tp + 1) // 2):
            order += [n_tp - 1 - c, c] if c != n_tp - 1 - c else [c]
        for c in order:
            part[c, rows, :] = jnp.dot(
                attn[...], w_ref[:, c * width:(c + 1) * width],
                preferred_element_type=jnp.float32).astype(jnp.bfloat16)
            if c >= 2:
                @pl.when(z == 0)
                def _():
                    right_copy(c, b).start()
            if c < n_tp - 2:
                @pl.when(z == n_tp - 1)
                def _():
                    left_copy(c, b).start()

    def forward_right(b):
        rows = pl.ds(pl.multiple_of(b * ROWS, ROWS), ROWS)
        for c in range(n_tp - 1, 1, -1):
            @pl.when(c > z)
            def _():
                copy = right_copy(c, b)
                copy.wait_recv()
                part[c, rows, :] = (part[c, rows, :].astype(jnp.float32)
                                    + recv_r[c, rows, :].astype(jnp.float32)).astype(jnp.bfloat16)
                copy.start()

    def forward_left(b):
        rows = pl.ds(pl.multiple_of(b * ROWS, ROWS), ROWS)
        for c in range(n_tp - 2):
            @pl.when(c < z)
            def _():
                copy = left_copy(c, b)
                copy.wait_recv()
                part[c, rows, :] = (part[c, rows, :].astype(jnp.float32)
                                    + recv_l[c, rows, :].astype(jnp.float32)).astype(jnp.bfloat16)
                copy.start()

    low_half = z < n_tp // 2
    middle = jnp.logical_and(z > 0, z < n_tp - 1)

    def step(b, carry):
        @pl.when(b < blocks)
        def _():
            compute(b)

        right_b = b - jnp.where(low_half, 1, 2)
        left_b = b - jnp.where(low_half, 2, 1)

        @pl.when(middle & low_half & (right_b >= 0) & (right_b < blocks))
        def _():
            forward_right(right_b)

        @pl.when(middle & (left_b >= 0) & (left_b < blocks))
        def _():
            forward_left(left_b)

        @pl.when(middle & jnp.logical_not(low_half) & (right_b >= 0) & (right_b < blocks))
        def _():
            forward_right(right_b)
        return carry

    lax.fori_loop(0, blocks + 2, step, 0)

    @pl.when(z == 0)
    def _():
        for b in range(blocks):
            for c in range(n_tp - 1, 1, -1):
                right_copy(c, b).wait_send()
            if b == blocks - 2:
                for late in range(blocks):
                    right_copy(1, late).start()

    @pl.when(z == n_tp - 1)
    def _():
        for b in range(blocks):
            for c in range(n_tp - 2):
                left_copy(c, b).wait_send()
            if b == blocks - 2:
                for late in range(blocks):
                    left_copy(n_tp - 2, late).start()

    def finish(b, carry):
        rows = pl.ds(pl.multiple_of(b * ROWS, ROWS), ROWS)

        @pl.when(z == 0)
        def _():
            left_copy(z, b).wait_recv()
            out_ref[rows, :] = (part[z, rows, :].astype(jnp.float32)
                                + recv_l[z, rows, :].astype(jnp.float32)).astype(out_ref.dtype)

        @pl.when(z == n_tp - 1)
        def _():
            right_copy(z, b).wait_recv()
            out_ref[rows, :] = (part[z, rows, :].astype(jnp.float32)
                                + recv_r[z, rows, :].astype(jnp.float32)).astype(out_ref.dtype)

        @pl.when(middle)
        def _():
            right_copy(z, b).wait_recv()
            left_copy(z, b).wait_recv()
            out_ref[rows, :] = (part[z, rows, :].astype(jnp.float32)
                                + recv_r[z, rows, :].astype(jnp.float32)
                                + recv_l[z, rows, :].astype(jnp.float32)).astype(out_ref.dtype)
        return carry

    lax.fori_loop(0, blocks, finish, 0)

    chip_each(1, lambda copy: copy.wait_send())
    for d in range(1, hops + 1):
        @pl.when(i + 2 * d < n_loop)
        def _():
            id_chip(d).wait_send()

        @pl.when((core == 1) & (i >= 2 * d))
        def _():
            id_down(d).wait_send()
            for t in range(2):
                down_copy(t, d).wait_send()

        @pl.when((core == 0) & (i >= 2 * d - 2))
        def _():
            id_up(d - 1).wait_send()
            for t in range(2):
                up_copy(t, d - 1).wait_send()
    if relay:
        @pl.when(chip == 3)
        def _():
            for t in range(2):
                relay_copy(t).wait_send()

    def drain(b, carry):
        @pl.when(z == 0)
        def _():
            right_copy(1, b).wait_send()

        @pl.when(z == n_tp - 1)
        def _():
            left_copy(n_tp - 2, b).wait_send()

        for c in range(n_tp):
            @pl.when(middle & (c > z))
            def _():
                right_copy(c, b).wait_send()

            @pl.when(middle & (c < z))
            def _():
                left_copy(c, b).wait_send()
        return carry

    lax.fori_loop(0, blocks, drain, 0)


def per_device(queries, key_values, prompt_ids, out_weight):
    n_loop, n_tp = lax.axis_size("loop"), lax.axis_size("tp")
    tok, q_cols = queries.shape
    depth, d_out = out_weight.shape
    width = d_out // n_tp
    reach = min(8, n_loop // 2)
    blocks = tok // ROWS
    hops = reach // 2
    vmem = pltpu.VMEM
    dma = pltpu.SemaphoreType.DMA
    any_spec = pl.BlockSpec(memory_space=pl.ANY)
    vmem_spec = pl.BlockSpec(memory_space=pltpu.VMEM)
    return pl.pallas_call(
        functools.partial(kernel, n_loop, n_tp, reach),
        out_shape=pltpu.VMEM((tok, width), jnp.bfloat16),
        in_specs=[any_spec] * 4,
        out_specs=vmem_spec,
        scratch_shapes=[
            vmem((tok, q_cols), jnp.bfloat16),
            vmem((reach + 1, tok, 2 * HD), jnp.bfloat16),
            vmem(((reach + 1) * tok, 2 * HD), jnp.bfloat16),
            vmem((reach + 1, 1, tok), jnp.int32),
            vmem((tok, 1), jnp.float32),
            vmem((ROWS, reach * tok), jnp.float32),
            vmem((q_cols // HD * ROWS, (reach + 1) * tok), jnp.bfloat16),
            vmem((ROWS, q_cols), jnp.bfloat16),
            vmem((depth, d_out), jnp.bfloat16),
            vmem((n_tp, tok, width), jnp.bfloat16),
            vmem((n_tp, tok, width), jnp.bfloat16),
            vmem((n_tp, tok, width), jnp.bfloat16),
            dma((4,)), dma((2, 2, hops)), dma((2, 2, hops)), dma((2,)), dma((2, hops)), dma((2, hops)),
            dma((reach,)), dma((reach,)),
            dma((n_tp, blocks)), dma((n_tp, blocks)), dma((n_tp, blocks)),
        ],
        compiler_params=pltpu.CompilerParams(
            collective_id=0, has_side_effects=True, vmem_limit_bytes=32 * 1024 * 1024),
        cost_estimate=pl.CostEstimate(flops=3_500_000_000, bytes_accessed=10_000_000, transcendentals=2_000_000),
    )(*(pltpu.with_memory_space_constraint(x, pltpu.HBM)
        for x in (queries, key_values, prompt_ids.reshape(1, tok), out_weight)))


def solution(mesh):
    in_specs = (P("loop", "tp"), P("loop", "tp"), P("loop"), P("tp", None))
    out_specs = P("loop", "tp")
    return jax.shard_map(
        per_device, mesh=mesh, in_specs=in_specs, out_specs=out_specs, check_vma=False
    )
```

```python
import functools
import math

import jax
import jax.numpy as jnp
from jax import lax
from jax.experimental import pallas as pl
from jax.experimental.pallas import tpu as pltpu
from jax.sharding import PartitionSpec as P

HD = 128
BLOCKED = -1e30
ROWS = 32
STACK = 4
MESH = pl.DeviceIdType.MESH


def kernel(n_loop, n_tp, reach, q_hbm, kv_hbm, ids_hbm, w_hbm, out_ref,
           q_ref, kv_buf, k_t, v_buf, id_buf, q_col, bias, attn, w_ref, part, recv_r, recv_l,
           load_sem, kv_send, kv_recv, id_send, id_recv, send_sem, r_sem, l_sem):
    tok = q_ref.shape[0]
    heads = q_ref.shape[1] // HD
    width = part.shape[2]
    blocks = tok // ROWS
    far_last = reach * tok
    scale = math.log2(math.e) / math.sqrt(HD)
    i = lax.axis_index("loop")
    z = lax.axis_index("tp")

    load_q = pltpu.make_async_copy(q_hbm, q_ref, load_sem.at[0])
    load_kv = pltpu.make_async_copy(kv_hbm, kv_buf.at[reach], load_sem.at[1])
    load_w = pltpu.make_async_copy(w_hbm, w_ref, load_sem.at[2])
    load_ids = pltpu.make_async_copy(ids_hbm, id_buf.at[reach], load_sem.at[3])
    load_ids.start()
    load_kv.start()
    load_q.start()
    load_w.start()

    core = lax.rem(i, 2)
    hops = reach // 2

    def chip_copies(d):
        slot = reach - 2 * d
        return [
            pltpu.make_async_remote_copy(
                src_ref=source, dst_ref=target.at[slot], send_sem=sends.at[d - 1],
                recv_sem=arrivals.at[2 * d - 1], device_id=(i + 2 * d, z), device_id_type=MESH)
            for source, target, sends, arrivals in (
                (ids_hbm, id_buf, id_send, id_recv), (kv_hbm, kv_buf, kv_send, kv_recv))]

    def up_copies(d):
        return [
            pltpu.make_async_remote_copy(
                src_ref=source if d == 0 else target.at[reach - 2 * d], dst_ref=target.at[reach - 2 * d - 1],
                send_sem=sends.at[hops + d], recv_sem=arrivals.at[2 * d],
                device_id=(i + 1, z), device_id_type=MESH)
            for source, target, sends, arrivals in (
                (ids_hbm, id_buf, id_send, id_recv), (kv_hbm, kv_buf, kv_send, kv_recv))]

    def down_copies(d):
        return [
            pltpu.make_async_remote_copy(
                src_ref=target.at[reach - 2 * d], dst_ref=target.at[reach - 2 * d + 1],
                send_sem=sends.at[hops + d - 1], recv_sem=arrivals.at[2 * d - 2],
                device_id=(i - 1, z), device_id_type=MESH)
            for target, sends, arrivals in ((id_buf, id_send, id_recv), (kv_buf, kv_send, kv_recv))]

    def right_copy(c, b):
        rows = pl.ds(pl.multiple_of(b * ROWS, ROWS), ROWS)
        return pltpu.make_async_remote_copy(
            src_ref=part.at[c, rows], dst_ref=recv_r.at[c, rows], send_sem=send_sem.at[c, b],
            recv_sem=r_sem.at[c, b], device_id=(i, z + 1), device_id_type=MESH)

    def left_copy(c, b):
        rows = pl.ds(pl.multiple_of(b * ROWS, ROWS), ROWS)
        return pltpu.make_async_remote_copy(
            src_ref=part.at[c, rows], dst_ref=recv_l.at[c, rows], send_sem=send_sem.at[c, b],
            recv_sem=l_sem.at[c, b], device_id=(i, z - 1), device_id_type=MESH)

    barrier = pltpu.get_barrier_semaphore()
    pl.semaphore_signal(barrier, inc=1, device_id=(i + 1 - 2 * core, z), device_id_type=MESH)
    for d in range(1, hops + 1):
        @pl.when(i + 2 * d < n_loop)
        def _():
            pl.semaphore_signal(barrier, inc=1, device_id=(i + 2 * d, z), device_id_type=MESH)

        @pl.when(i - 2 * d >= 0)
        def _():
            pl.semaphore_signal(barrier, inc=1, device_id=(i - 2 * d, z), device_id_type=MESH)

    @pl.when(z > 0)
    def _():
        pl.semaphore_signal(barrier, inc=1, device_id=(i, z - 1), device_id_type=MESH)

    @pl.when(z < n_tp - 1)
    def _():
        pl.semaphore_signal(barrier, inc=1, device_id=(i, z + 1), device_id_type=MESH)

    chip = i // 2
    greeted = (1 + jnp.minimum(chip, hops) + jnp.minimum(n_loop // 2 - 1 - chip, hops)
               + jnp.minimum(z, 1) + jnp.minimum(n_tp - 1 - z, 1))
    pl.semaphore_wait(barrier, greeted)

    for d in range(1, hops + 1):
        @pl.when(i + 2 * d < n_loop)
        def _():
            for copy in chip_copies(d):
                copy.start()

    @pl.when(core == 0)
    def _():
        for copy in up_copies(0):
            copy.start()

    for k in range(1, reach + 1):
        @pl.when(i < k)
        def _():
            kv_buf[reach - k] = jnp.zeros(kv_buf.shape[1:], kv_buf.dtype)
            id_buf[reach - k] = jnp.full(id_buf.shape[1:], -1, id_buf.dtype)
    load_ids.wait()
    own_ids = id_buf[reach].astype(jnp.float32)
    square = (tok, tok)
    q_col[...] = jnp.max(
        jnp.where(lax.broadcasted_iota(jnp.int32, square, 0) == lax.broadcasted_iota(jnp.int32, square, 1),
                  jnp.broadcast_to(own_ids, square), -1.0), axis=1, keepdims=True)
    v_buf[:, HD:] = jnp.ones((v_buf.shape[0], HD), v_buf.dtype)
    load_kv.wait()
    load_q.wait()
    for d in range(1, hops + 1):
        @pl.when(i >= 2 * d)
        def _():
            for copy in chip_copies(d):
                copy.wait_recv()

            @pl.when(core == 1)
            def _():
                for copy in down_copies(d):
                    copy.start()

            if d < hops:
                @pl.when(core == 0)
                def _():
                    for copy in up_copies(d):
                        copy.start()
    for d in range(1, hops + 1):
        @pl.when((core == 0) & (i >= 2 * d))
        def _():
            for copy in down_copies(d):
                copy.wait_recv()

        @pl.when((core == 1) & (i >= 2 * d - 1))
        def _():
            for copy in up_copies(d - 1):
                copy.wait_recv()
    for s in range(reach + 1):
        k_t[:, s * tok:(s + 1) * tok] = kv_buf[s, :, :HD].T
        v_buf[s * tok:(s + 1) * tok, :HD] = kv_buf[s, :, HD:]

    low_half = z < n_tp // 2

    def compute(b):
        rows = pl.ds(pl.multiple_of(b * ROWS, ROWS), ROWS)
        q_ids = q_col[rows, :]
        shape = (ROWS, tok)
        lower = (lax.broadcasted_iota(jnp.int32, shape, 1)
                 <= lax.broadcasted_iota(jnp.int32, shape, 0) + b * ROWS)
        key_ids = [jnp.broadcast_to(id_buf[s].astype(jnp.float32), shape) for s in range(reach + 1)]
        shared = jnp.where(lower, key_ids[reach], key_ids[0])
        for s, ids in enumerate([shared] + key_ids[1:reach]):
            bias[:, s * tok:(s + 1) * tok] = jnp.where(ids == q_ids, 0.0, BLOCKED)
        for h in range(0, heads, STACK):
            q = jnp.concatenate([q_ref[rows, (h + j) * HD:(h + j + 1) * HD] for j in range(STACK)], axis=0)
            s = jnp.dot(q, k_t[...], preferred_element_type=jnp.float32)
            s = s.reshape(STACK, ROWS, (reach + 1) * tok)
            s = jnp.concatenate(
                [jnp.where(lower[None], s[:, :, far_last:], s[:, :, :tok]), s[:, :, tok:far_last]], axis=2)
            s = s * scale + bias[...][None]
            p = jnp.exp2(s - jnp.max(s, axis=2, keepdims=True))
            first = p[:, :, :tok]
            p = jnp.concatenate(
                [jnp.where(lower[None], 0.0, first), p[:, :, tok:], jnp.where(lower[None], first, 0.0)], axis=2)
            p = p.reshape(STACK * ROWS, (reach + 1) * tok).astype(jnp.bfloat16)
            o = jnp.dot(p, v_buf[...], preferred_element_type=jnp.float32)
            o = (o[:, :HD] / o[:, HD:]).astype(jnp.bfloat16)
            for j in range(STACK):
                attn[rows, (h + j) * HD:(h + j + 1) * HD] = o[j * ROWS:(j + 1) * ROWS]

        @pl.when(b == 0)
        def _():
            load_w.wait()

    def project(b, count):
        rows = pl.ds(pl.multiple_of(b * ROWS, ROWS), count * ROWS)
        heads_out = attn[rows, :]

        def one(j, carry):
            c = jnp.where(low_half, n_tp - 1 - j, j)
            part[c, rows, :] = jnp.dot(
                heads_out, w_ref[:, pl.ds(pl.multiple_of(c * width, width), width)],
                preferred_element_type=jnp.float32).astype(jnp.bfloat16)

            @pl.when((z == 0) & (c >= 2))
            def _():
                for n in range(count):
                    right_copy(c, b + n).start()

            @pl.when((z == n_tp - 1) & (c < n_tp - 2))
            def _():
                for n in range(count):
                    left_copy(c, b + n).start()
            return carry

        lax.fori_loop(0, n_tp, one, 0)

    def forward_right(b):
        rows = pl.ds(pl.multiple_of(b * ROWS, ROWS), ROWS)
        for c in range(n_tp - 1, 1, -1):
            @pl.when(c > z)
            def _():
                copy = right_copy(c, b)
                copy.wait_recv()
                part[c, rows, :] = (part[c, rows, :].astype(jnp.float32)
                                    + recv_r[c, rows, :].astype(jnp.float32)).astype(jnp.bfloat16)
                copy.start()

    def forward_left(b):
        rows = pl.ds(pl.multiple_of(b * ROWS, ROWS), ROWS)
        for c in range(n_tp - 2):
            @pl.when(c < z)
            def _():
                copy = left_copy(c, b)
                copy.wait_recv()
                part[c, rows, :] = (part[c, rows, :].astype(jnp.float32)
                                    + recv_l[c, rows, :].astype(jnp.float32)).astype(jnp.bfloat16)
                copy.start()

    middle = jnp.logical_and(z > 0, z < n_tp - 1)

    def step(b, carry):
        @pl.when(b < blocks)
        def _():
            compute(b)

        @pl.when(b < 2)
        def _():
            project(b, 1)

        @pl.when((b < blocks) & (b > 2) & (b % 2 == 1))
        def _():
            project(b - 1, 2)

        late = b - blocks // 2

        @pl.when((z == 0) & (late >= 0) & (b < blocks))
        def _():
            right_copy(1, late).start()

        @pl.when((z == n_tp - 1) & (late >= 0) & (b < blocks))
        def _():
            left_copy(n_tp - 2, late).start()

        right_b = b - jnp.where(low_half, 1, 2)
        left_b = b - jnp.where(low_half, 2, 1)

        @pl.when(middle & low_half & (right_b >= 0) & (right_b < blocks))
        def _():
            forward_right(right_b)

        @pl.when(middle & (left_b >= 0) & (left_b < blocks))
        def _():
            forward_left(left_b)

        @pl.when(middle & jnp.logical_not(low_half) & (right_b >= 0) & (right_b < blocks))
        def _():
            forward_right(right_b)
        return carry

    lax.fori_loop(0, blocks + 2, step, 0)

    @pl.when(z == 0)
    def _():
        for b in range(blocks):
            for c in range(n_tp - 1, 1, -1):
                right_copy(c, b).wait_send()
            if b == blocks - 2:
                for late in range(blocks // 2, blocks):
                    right_copy(1, late).start()

    @pl.when(z == n_tp - 1)
    def _():
        for b in range(blocks):
            for c in range(n_tp - 2):
                left_copy(c, b).wait_send()
            if b == blocks - 2:
                for late in range(blocks // 2, blocks):
                    left_copy(n_tp - 2, late).start()

    def finish(b, carry):
        rows = pl.ds(pl.multiple_of(b * ROWS, ROWS), ROWS)

        @pl.when(z == 0)
        def _():
            left_copy(z, b).wait_recv()
            out_ref[rows, :] = (part[z, rows, :].astype(jnp.float32)
                                + recv_l[z, rows, :].astype(jnp.float32)).astype(out_ref.dtype)

        @pl.when(z == n_tp - 1)
        def _():
            right_copy(z, b).wait_recv()
            out_ref[rows, :] = (part[z, rows, :].astype(jnp.float32)
                                + recv_r[z, rows, :].astype(jnp.float32)).astype(out_ref.dtype)

        @pl.when(middle)
        def _():
            right_copy(z, b).wait_recv()
            left_copy(z, b).wait_recv()
            out_ref[rows, :] = (part[z, rows, :].astype(jnp.float32)
                                + recv_r[z, rows, :].astype(jnp.float32)
                                + recv_l[z, rows, :].astype(jnp.float32)).astype(out_ref.dtype)
        return carry

    lax.fori_loop(0, blocks, finish, 0)

    for d in range(1, hops + 1):
        @pl.when(i + 2 * d < n_loop)
        def _():
            for copy in chip_copies(d):
                copy.wait_send()

        @pl.when((core == 1) & (i >= 2 * d))
        def _():
            for copy in down_copies(d):
                copy.wait_send()

        @pl.when((core == 0) & (i >= 2 * d - 2))
        def _():
            for copy in up_copies(d - 1):
                copy.wait_send()

    def drain(b, carry):
        @pl.when(z == 0)
        def _():
            right_copy(1, b).wait_send()

        @pl.when(z == n_tp - 1)
        def _():
            left_copy(n_tp - 2, b).wait_send()

        for c in range(n_tp):
            @pl.when(middle & (c > z))
            def _():
                right_copy(c, b).wait_send()

            @pl.when(middle & (c < z))
            def _():
                left_copy(c, b).wait_send()
        return carry

    lax.fori_loop(0, blocks, drain, 0)


def per_device(queries, key_values, prompt_ids, out_weight):
    n_loop, n_tp = lax.axis_size("loop"), lax.axis_size("tp")
    tok, q_cols = queries.shape
    depth, d_out = out_weight.shape
    width = d_out // n_tp
    reach = min(8, n_loop // 2)
    blocks = tok // ROWS
    vmem = pltpu.VMEM
    dma = pltpu.SemaphoreType.DMA
    any_spec = pl.BlockSpec(memory_space=pl.ANY)
    vmem_spec = pl.BlockSpec(memory_space=pltpu.VMEM)
    return pl.pallas_call(
        functools.partial(kernel, n_loop, n_tp, reach),
        out_shape=pltpu.VMEM((tok, width), jnp.bfloat16),
        in_specs=[any_spec] * 4,
        out_specs=vmem_spec,
        scratch_shapes=[
            vmem((tok, q_cols), jnp.bfloat16),
            vmem((reach + 1, tok, 2 * HD), jnp.bfloat16),
            vmem((HD, (reach + 1) * tok), jnp.bfloat16),
            vmem(((reach + 1) * tok, 2 * HD), jnp.bfloat16),
            vmem((reach + 1, 1, tok), jnp.int32),
            vmem((tok, 1), jnp.float32),
            vmem((ROWS, reach * tok), jnp.float32),
            vmem((tok, q_cols), jnp.bfloat16),
            vmem((depth, d_out), jnp.bfloat16),
            vmem((n_tp, tok, width), jnp.bfloat16),
            vmem((n_tp, tok, width), jnp.bfloat16),
            vmem((n_tp, tok, width), jnp.bfloat16),
            dma((4,)), dma((reach,)), dma((reach,)), dma((reach,)), dma((reach,)),
            dma((n_tp, blocks)), dma((n_tp, blocks)), dma((n_tp, blocks)),
        ],
        compiler_params=pltpu.CompilerParams(
            collective_id=0, has_side_effects=True, vmem_limit_bytes=32 * 1024 * 1024),
        cost_estimate=pl.CostEstimate(flops=3_500_000_000, bytes_accessed=10_000_000, transcendentals=2_000_000),
    )(*(pltpu.with_memory_space_constraint(x, pltpu.HBM)
        for x in (queries, key_values, prompt_ids.reshape(1, tok), out_weight)))


def solution(mesh):
    in_specs = (P("loop", "tp"), P("loop", "tp"), P("loop"), P("tp", None))
    out_specs = P("loop", "tp")
    return jax.shard_map(
        per_device, mesh=mesh, in_specs=in_specs, out_specs=out_specs, check_vma=False
    )
```

```python
import functools
import math

import jax
import jax.numpy as jnp
from jax import lax
from jax.experimental import pallas as pl
from jax.experimental.pallas import tpu as pltpu
from jax.sharding import PartitionSpec as P

HD = 128
BLOCKED = -1e30
ROWS = 32
STACK = 4
MESH = pl.DeviceIdType.MESH


def kernel(n_loop, n_tp, reach, q_hbm, kv_hbm, ids_hbm, w_hbm, out_ref,
           q_ref, kv_buf, v_buf, id_buf, q_col, bias, attn, w_ref, part, recv_r, recv_l,
           load_sem, w_sem, kv_send, kv_recv, chip_send, chip_recv, relay_send, id_send, id_recv, send_sem, r_sem, l_sem):
    tok = q_ref.shape[0]
    heads = q_ref.shape[1] // HD
    width = part.shape[2]
    blocks = tok // ROWS
    far_last = reach * tok
    scale = math.log2(math.e) / math.sqrt(HD)
    i = lax.axis_index("loop")
    z = lax.axis_index("tp")

    load_q = pltpu.make_async_copy(q_hbm, q_ref, load_sem.at[0])
    load_kv = pltpu.make_async_copy(kv_hbm, kv_buf.at[reach], load_sem.at[1])
    low_half = z < n_tp // 2

    def load_w(j):
        c = jnp.where(low_half, n_tp - 1 - j, j)
        cols = pl.ds(pl.multiple_of(c * width, width), width)
        return pltpu.make_async_copy(w_hbm.at[:, cols], w_ref.at[:, cols], w_sem.at[j])

    load_ids = pltpu.make_async_copy(ids_hbm, id_buf.at[reach], load_sem.at[2])
    load_ids.start()
    load_kv.start()
    load_q.start()
    for j in range(n_tp):
        load_w(j).start()

    core = lax.rem(i, 2)
    chip = i // 2
    hops = reach // 2

    half = tok // 2
    relay = n_loop == 8 and hops == 2

    def id_chip(d):
        return pltpu.make_async_remote_copy(
            src_ref=ids_hbm, dst_ref=id_buf.at[reach - 2 * d], send_sem=id_send.at[d - 1],
            recv_sem=id_recv.at[2 * d - 1], device_id=(i + 2 * d, z), device_id_type=MESH)

    def kv_chip(h, d):
        rows = pl.ds(h * half, half)
        return pltpu.make_async_remote_copy(
            src_ref=kv_hbm.at[rows], dst_ref=kv_buf.at[reach - 2 * d, rows],
            send_sem=chip_send.at[h, d - 1], recv_sem=chip_recv.at[h, d - 1],
            device_id=(i + 2 * d, z), device_id_type=MESH)

    def kv_relay():
        rows = pl.ds(0, half)
        return pltpu.make_async_remote_copy(
            src_ref=kv_buf.at[reach - 4, rows], dst_ref=kv_buf.at[reach - 2, rows],
            send_sem=relay_send.at[0], recv_sem=chip_recv.at[0, 0],
            device_id=(i - 2, z), device_id_type=MESH)

    def chip_each(act):
        for h in range(2):
            for d in range(hops, 0, -1):
                there = i + 2 * d < n_loop
                if relay and h == 0 and d == 1:
                    there = there & (chip != 1)

                @pl.when(there)
                def _():
                    act(kv_chip(h, d))

    def up_copies(d):
        return [
            pltpu.make_async_remote_copy(
                src_ref=source if d == 0 else target.at[reach - 2 * d], dst_ref=target.at[reach - 2 * d - 1],
                send_sem=sends.at[hops + d], recv_sem=arrivals.at[2 * d],
                device_id=(i + 1, z), device_id_type=MESH)
            for source, target, sends, arrivals in (
                (ids_hbm, id_buf, id_send, id_recv), (kv_hbm, kv_buf, kv_send, kv_recv))]

    def down_copies(d):
        return [
            pltpu.make_async_remote_copy(
                src_ref=target.at[reach - 2 * d], dst_ref=target.at[reach - 2 * d + 1],
                send_sem=sends.at[hops + d - 1], recv_sem=arrivals.at[2 * d - 2],
                device_id=(i - 1, z), device_id_type=MESH)
            for target, sends, arrivals in ((id_buf, id_send, id_recv), (kv_buf, kv_send, kv_recv))]

    def right_copy(c, b):
        rows = pl.ds(pl.multiple_of(b * ROWS, ROWS), ROWS)
        return pltpu.make_async_remote_copy(
            src_ref=part.at[c, rows], dst_ref=recv_r.at[c, rows], send_sem=send_sem.at[c, b],
            recv_sem=r_sem.at[c, b], device_id=(i, z + 1), device_id_type=MESH)

    def left_copy(c, b):
        rows = pl.ds(pl.multiple_of(b * ROWS, ROWS), ROWS)
        return pltpu.make_async_remote_copy(
            src_ref=part.at[c, rows], dst_ref=recv_l.at[c, rows], send_sem=send_sem.at[c, b],
            recv_sem=l_sem.at[c, b], device_id=(i, z - 1), device_id_type=MESH)

    barrier = pltpu.get_barrier_semaphore()
    pl.semaphore_signal(barrier, inc=1, device_id=(i + 1 - 2 * core, z), device_id_type=MESH)
    for d in range(1, hops + 1):
        @pl.when(i + 2 * d < n_loop)
        def _():
            pl.semaphore_signal(barrier, inc=1, device_id=(i + 2 * d, z), device_id_type=MESH)

        @pl.when(i - 2 * d >= 0)
        def _():
            pl.semaphore_signal(barrier, inc=1, device_id=(i - 2 * d, z), device_id_type=MESH)

    @pl.when(z > 0)
    def _():
        pl.semaphore_signal(barrier, inc=1, device_id=(i, z - 1), device_id_type=MESH)

    @pl.when(z < n_tp - 1)
    def _():
        pl.semaphore_signal(barrier, inc=1, device_id=(i, z + 1), device_id_type=MESH)

    greeted = (1 + jnp.minimum(chip, hops) + jnp.minimum(n_loop // 2 - 1 - chip, hops)
               + jnp.minimum(z, 1) + jnp.minimum(n_tp - 1 - z, 1))
    pl.semaphore_wait(barrier, greeted)

    for d in range(1, hops + 1):
        @pl.when(i + 2 * d < n_loop)
        def _():
            id_chip(d).start()

    chip_each(lambda copy: copy.start())

    @pl.when(core == 0)
    def _():
        for copy in up_copies(0):
            copy.start()

    for k in range(1, reach + 1):
        @pl.when(i < k)
        def _():
            kv_buf[reach - k] = jnp.zeros(kv_buf.shape[1:], kv_buf.dtype)
            id_buf[reach - k] = jnp.full(id_buf.shape[1:], -1, id_buf.dtype)
    load_ids.wait()
    own_ids = id_buf[reach].astype(jnp.float32)
    square = (tok, tok)
    q_col[...] = jnp.max(
        jnp.where(lax.broadcasted_iota(jnp.int32, square, 0) == lax.broadcasted_iota(jnp.int32, square, 1),
                  jnp.broadcast_to(own_ids, square), -1.0), axis=1, keepdims=True)
    v_buf[:, HD:] = jnp.ones((v_buf.shape[0], HD), v_buf.dtype)
    load_kv.wait()
    load_q.wait()
    for d in range(hops, 0, -1):
        @pl.when(i >= 2 * d)
        def _():
            id_chip(d).wait_recv()
            kv_chip(0, d).wait_recv()
            if relay and d == 2:
                @pl.when(chip == 3)
                def _():
                    kv_relay().start()
            kv_chip(1, d).wait_recv()

            @pl.when(core == 1)
            def _():
                for copy in down_copies(d):
                    copy.start()

            if d < hops:
                @pl.when(core == 0)
                def _():
                    for copy in up_copies(d):
                        copy.start()
    for d in range(1, hops + 1):
        @pl.when((core == 0) & (i >= 2 * d))
        def _():
            for copy in down_copies(d):
                copy.wait_recv()

        @pl.when((core == 1) & (i >= 2 * d - 1))
        def _():
            for copy in up_copies(d - 1):
                copy.wait_recv()
    for s in range(reach + 1):
        v_buf[s * tok:(s + 1) * tok, :HD] = kv_buf[s, :, HD:]

    def compute(b):
        rows = pl.ds(pl.multiple_of(b * ROWS, ROWS), ROWS)
        q_ids = q_col[rows, :]
        shape = (ROWS, tok)
        lower = (lax.broadcasted_iota(jnp.int32, shape, 1)
                 <= lax.broadcasted_iota(jnp.int32, shape, 0) + b * ROWS)
        key_ids = [jnp.broadcast_to(id_buf[s].astype(jnp.float32), shape) for s in range(reach + 1)]
        shared = jnp.where(lower, key_ids[reach], key_ids[0])
        for s, ids in enumerate([shared] + key_ids[1:reach]):
            bias[:, s * tok:(s + 1) * tok] = jnp.where(ids == q_ids, 0.0, BLOCKED)
        keys = kv_buf[:, :, :HD].reshape((reach + 1) * tok, HD)
        for h in range(0, heads, STACK):
            q = jnp.concatenate([q_ref[rows, (h + j) * HD:(h + j + 1) * HD] for j in range(STACK)], axis=0)
            s = lax.dot_general(q, keys, (((1,), (1,)), ((), ())), preferred_element_type=jnp.float32)
            s = s.reshape(STACK, ROWS, (reach + 1) * tok)
            s = jnp.concatenate(
                [jnp.where(lower[None], s[:, :, far_last:], s[:, :, :tok]), s[:, :, tok:far_last]], axis=2)
            s = s * scale + bias[...][None]
            p = jnp.exp2(s - jnp.max(s, axis=2, keepdims=True))
            first = p[:, :, :tok]
            p = jnp.concatenate(
                [jnp.where(lower[None], 0.0, first), p[:, :, tok:], jnp.where(lower[None], first, 0.0)], axis=2)
            p = p.reshape(STACK * ROWS, (reach + 1) * tok).astype(jnp.bfloat16)
            o = jnp.dot(p, v_buf[...], preferred_element_type=jnp.float32)
            o = (o[:, :HD] / o[:, HD:]).astype(jnp.bfloat16)
            for j in range(STACK):
                attn[:, (h + j) * HD:(h + j + 1) * HD] = o[j * ROWS:(j + 1) * ROWS]

        for j in range(n_tp):
            c = jnp.where(low_half, n_tp - 1 - j, j)

            @pl.when(b == 0)
            def _():
                load_w(j).wait()

            part[c, rows, :] = jnp.dot(
                attn[...], w_ref[:, pl.ds(pl.multiple_of(c * width, width), width)],
                preferred_element_type=jnp.float32).astype(jnp.bfloat16)

            @pl.when((z == 0) & (c >= 2))
            def _():
                right_copy(c, b).start()

            @pl.when((z == n_tp - 1) & (c < n_tp - 2))
            def _():
                left_copy(c, b).start()

    def forward_right(b):
        rows = pl.ds(pl.multiple_of(b * ROWS, ROWS), ROWS)
        for c in range(n_tp - 1, 1, -1):
            @pl.when(c > z)
            def _():
                copy = right_copy(c, b)
                copy.wait_recv()
                part[c, rows, :] = (part[c, rows, :].astype(jnp.float32)
                                    + recv_r[c, rows, :].astype(jnp.float32)).astype(jnp.bfloat16)
                copy.start()

    def forward_left(b):
        rows = pl.ds(pl.multiple_of(b * ROWS, ROWS), ROWS)
        for c in range(n_tp - 2):
            @pl.when(c < z)
            def _():
                copy = left_copy(c, b)
                copy.wait_recv()
                part[c, rows, :] = (part[c, rows, :].astype(jnp.float32)
                                    + recv_l[c, rows, :].astype(jnp.float32)).astype(jnp.bfloat16)
                copy.start()

    middle = jnp.logical_and(z > 0, z < n_tp - 1)

    def step(b, carry):
        @pl.when(b < blocks)
        def _():
            compute(b)

        right_b = b - jnp.where(low_half, 1, 2)
        left_b = b - jnp.where(low_half, 2, 1)

        @pl.when(middle & low_half & (right_b >= 0) & (right_b < blocks))
        def _():
            forward_right(right_b)

        @pl.when(middle & (left_b >= 0) & (left_b < blocks))
        def _():
            forward_left(left_b)

        @pl.when(middle & jnp.logical_not(low_half) & (right_b >= 0) & (right_b < blocks))
        def _():
            forward_right(right_b)
        return carry

    lax.fori_loop(0, blocks + 2, step, 0)

    @pl.when(z == 0)
    def _():
        for b in range(blocks):
            for c in range(n_tp - 1, 1, -1):
                right_copy(c, b).wait_send()
            if b == blocks - 2:
                for late in range(blocks):
                    right_copy(1, late).start()

    @pl.when(z == n_tp - 1)
    def _():
        for b in range(blocks):
            for c in range(n_tp - 2):
                left_copy(c, b).wait_send()
            if b == blocks - 2:
                for late in range(blocks):
                    left_copy(n_tp - 2, late).start()

    def finish(b, carry):
        rows = pl.ds(pl.multiple_of(b * ROWS, ROWS), ROWS)

        @pl.when(z == 0)
        def _():
            left_copy(z, b).wait_recv()
            out_ref[rows, :] = (part[z, rows, :].astype(jnp.float32)
                                + recv_l[z, rows, :].astype(jnp.float32)).astype(out_ref.dtype)

        @pl.when(z == n_tp - 1)
        def _():
            right_copy(z, b).wait_recv()
            out_ref[rows, :] = (part[z, rows, :].astype(jnp.float32)
                                + recv_r[z, rows, :].astype(jnp.float32)).astype(out_ref.dtype)

        @pl.when(middle)
        def _():
            right_copy(z, b).wait_recv()
            left_copy(z, b).wait_recv()
            out_ref[rows, :] = (part[z, rows, :].astype(jnp.float32)
                                + recv_r[z, rows, :].astype(jnp.float32)
                                + recv_l[z, rows, :].astype(jnp.float32)).astype(out_ref.dtype)
        return carry

    lax.fori_loop(0, blocks, finish, 0)

    chip_each(lambda copy: copy.wait_send())
    if relay:
        @pl.when(chip == 3)
        def _():
            kv_relay().wait_send()
    for d in range(1, hops + 1):
        @pl.when(i + 2 * d < n_loop)
        def _():
            id_chip(d).wait_send()

        @pl.when((core == 1) & (i >= 2 * d))
        def _():
            for copy in down_copies(d):
                copy.wait_send()

        @pl.when((core == 0) & (i >= 2 * d - 2))
        def _():
            for copy in up_copies(d - 1):
                copy.wait_send()

    def drain(b, carry):
        @pl.when(z == 0)
        def _():
            right_copy(1, b).wait_send()

        @pl.when(z == n_tp - 1)
        def _():
            left_copy(n_tp - 2, b).wait_send()

        for c in range(n_tp):
            @pl.when(middle & (c > z))
            def _():
                right_copy(c, b).wait_send()

            @pl.when(middle & (c < z))
            def _():
                left_copy(c, b).wait_send()
        return carry

    lax.fori_loop(0, blocks, drain, 0)


def per_device(queries, key_values, prompt_ids, out_weight):
    n_loop, n_tp = lax.axis_size("loop"), lax.axis_size("tp")
    tok, q_cols = queries.shape
    depth, d_out = out_weight.shape
    width = d_out // n_tp
    reach = min(8, n_loop // 2)
    blocks = tok // ROWS
    hops = reach // 2
    vmem = pltpu.VMEM
    dma = pltpu.SemaphoreType.DMA
    any_spec = pl.BlockSpec(memory_space=pl.ANY)
    vmem_spec = pl.BlockSpec(memory_space=pltpu.VMEM)
    return pl.pallas_call(
        functools.partial(kernel, n_loop, n_tp, reach),
        out_shape=pltpu.VMEM((tok, width), jnp.bfloat16),
        in_specs=[any_spec] * 4,
        out_specs=vmem_spec,
        scratch_shapes=[
            vmem((tok, q_cols), jnp.bfloat16),
            vmem((reach + 1, tok, 2 * HD), jnp.bfloat16),
            vmem(((reach + 1) * tok, 2 * HD), jnp.bfloat16),
            vmem((reach + 1, 1, tok), jnp.int32),
            vmem((tok, 1), jnp.float32),
            vmem((ROWS, reach * tok), jnp.float32),
            vmem((ROWS, q_cols), jnp.bfloat16),
            vmem((depth, d_out), jnp.bfloat16),
            vmem((n_tp, tok, width), jnp.bfloat16),
            vmem((n_tp, tok, width), jnp.bfloat16),
            vmem((n_tp, tok, width), jnp.bfloat16),
            dma((3,)), dma((n_tp,)), dma((reach,)), dma((reach,)), dma((2, hops)), dma((2, hops)), dma((1,)),
            dma((reach,)), dma((reach,)),
            dma((n_tp, blocks)), dma((n_tp, blocks)), dma((n_tp, blocks)),
        ],
        compiler_params=pltpu.CompilerParams(
            collective_id=0, has_side_effects=True, vmem_limit_bytes=32 * 1024 * 1024),
        cost_estimate=pl.CostEstimate(flops=3_500_000_000, bytes_accessed=10_000_000, transcendentals=2_000_000),
    )(*(pltpu.with_memory_space_constraint(x, pltpu.HBM)
        for x in (queries, key_values, prompt_ids.reshape(1, tok), out_weight)))


def solution(mesh):
    in_specs = (P("loop", "tp"), P("loop", "tp"), P("loop"), P("tp", None))
    out_specs = P("loop", "tp")
    return jax.shard_map(
        per_device, mesh=mesh, in_specs=in_specs, out_specs=out_specs, check_vma=False
    )
```

```python
import functools
import math

import jax
import jax.numpy as jnp
from jax import lax
from jax.experimental import pallas as pl
from jax.experimental.pallas import tpu as pltpu
from jax.sharding import PartitionSpec as P

HD = 128
BLOCKED = -1e30
ROWS = 32
STACK = 4
MESH = pl.DeviceIdType.MESH


def kernel(n_loop, n_tp, reach, q_hbm, kv_hbm, ids_hbm, w_hbm, out_ref,
           q_ref, kv_buf, v_buf, id_buf, q_col, bias, attn, w_ref, part, recv_r, recv_l, side_a, side_b,
           load_sem, w_sem, kv_send, kv_recv, chip_send, chip_recv, side_sem, id_send, id_recv, send_sem, r_sem, l_sem):
    tok = q_ref.shape[0]
    heads = q_ref.shape[1] // HD
    width = part.shape[2]
    blocks = tok // ROWS
    far_last = reach * tok
    scale = math.log2(math.e) / math.sqrt(HD)
    i = lax.axis_index("loop")
    z = lax.axis_index("tp")

    load_q = pltpu.make_async_copy(q_hbm, q_ref, load_sem.at[0])
    load_kv = pltpu.make_async_copy(kv_hbm, kv_buf.at[reach], load_sem.at[1])
    low_half = z < n_tp // 2

    def load_w(j):
        c = jnp.where(low_half, n_tp - 1 - j, j)
        cols = pl.ds(pl.multiple_of(c * width, width), width)
        return pltpu.make_async_copy(w_hbm.at[:, cols], w_ref.at[:, cols], w_sem.at[j])

    load_ids = pltpu.make_async_copy(ids_hbm, id_buf.at[reach], load_sem.at[2])
    load_ids.start()
    load_kv.start()
    load_q.start()
    for j in range(n_tp):
        load_w(j).start()

    core = lax.rem(i, 2)
    chip = i // 2
    hops = reach // 2

    half = tok // 2

    def id_chip(d):
        return pltpu.make_async_remote_copy(
            src_ref=ids_hbm, dst_ref=id_buf.at[reach - 2 * d], send_sem=id_send.at[d - 1],
            recv_sem=id_recv.at[2 * d - 1], device_id=(i + 2 * d, z), device_id_type=MESH)

    def kv_chip(h, d):
        rows = pl.ds(h * half, half)
        return pltpu.make_async_remote_copy(
            src_ref=kv_hbm.at[rows], dst_ref=kv_buf.at[reach - 2 * d, rows],
            send_sem=chip_send.at[h, d - 1], recv_sem=chip_recv.at[h, d - 1],
            device_id=(i + 2 * d, z), device_id_type=MESH)

    def chip_each(act):
        for h in range(2):
            for d in range(hops, 0, -1):
                @pl.when(i + 2 * d < n_loop)
                def _():
                    act(kv_chip(h, d))

    def up_copies(d):
        return [
            pltpu.make_async_remote_copy(
                src_ref=source if d == 0 else target.at[reach - 2 * d], dst_ref=target.at[reach - 2 * d - 1],
                send_sem=sends.at[hops + d], recv_sem=arrivals.at[2 * d],
                device_id=(i + 1, z), device_id_type=MESH)
            for source, target, sends, arrivals in (
                (ids_hbm, id_buf, id_send, id_recv), (kv_hbm, kv_buf, kv_send, kv_recv))]

    def down_copies(d):
        return [
            pltpu.make_async_remote_copy(
                src_ref=target.at[reach - 2 * d], dst_ref=target.at[reach - 2 * d + 1],
                send_sem=sends.at[hops + d - 1], recv_sem=arrivals.at[2 * d - 2],
                device_id=(i - 1, z), device_id_type=MESH)
            for target, sends, arrivals in ((id_buf, id_send, id_recv), (kv_buf, kv_send, kv_recv))]

    def right_copy(c, b):
        rows = pl.ds(pl.multiple_of(b * ROWS, ROWS), ROWS)
        return pltpu.make_async_remote_copy(
            src_ref=part.at[c, rows], dst_ref=recv_r.at[c, rows], send_sem=send_sem.at[c, b],
            recv_sem=r_sem.at[c, b], device_id=(i, z + 1), device_id_type=MESH)

    def left_copy(c, b):
        rows = pl.ds(pl.multiple_of(b * ROWS, ROWS), ROWS)
        return pltpu.make_async_remote_copy(
            src_ref=part.at[c, rows], dst_ref=recv_l.at[c, rows], send_sem=send_sem.at[c, b],
            recv_sem=l_sem.at[c, b], device_id=(i, z - 1), device_id_type=MESH)

    side = n_loop == 8 and n_tp >= 4 and reach == 4
    given = 2 if side else 0

    def side_first(c, b):
        return pltpu.make_async_remote_copy(
            src_ref=part.at[c, pl.ds(b * ROWS, ROWS)], dst_ref=side_a.at[b], send_sem=side_sem.at[0, b],
            recv_sem=side_sem.at[1, b], device_id=(i - 4, z), device_id_type=MESH)

    def side_second(step, b):
        return pltpu.make_async_remote_copy(
            src_ref=side_a.at[b], dst_ref=side_b.at[b], send_sem=side_sem.at[2, b],
            recv_sem=side_sem.at[3, b], device_id=(i, z + step), device_id_type=MESH)

    def side_third(c, target, sems, b):
        return pltpu.make_async_remote_copy(
            src_ref=side_b.at[b], dst_ref=target.at[c, pl.ds(b * ROWS, ROWS)], send_sem=side_sem.at[4, b],
            recv_sem=sems.at[c, b], device_id=(i + 4, z), device_id_type=MESH)

    barrier = pltpu.get_barrier_semaphore()
    pl.semaphore_signal(barrier, inc=1, device_id=(i + 1 - 2 * core, z), device_id_type=MESH)
    for d in range(1, hops + 1):
        @pl.when(i + 2 * d < n_loop)
        def _():
            pl.semaphore_signal(barrier, inc=1, device_id=(i + 2 * d, z), device_id_type=MESH)

        @pl.when(i - 2 * d >= 0)
        def _():
            pl.semaphore_signal(barrier, inc=1, device_id=(i - 2 * d, z), device_id_type=MESH)

    @pl.when(z > 0)
    def _():
        pl.semaphore_signal(barrier, inc=1, device_id=(i, z - 1), device_id_type=MESH)

    @pl.when(z < n_tp - 1)
    def _():
        pl.semaphore_signal(barrier, inc=1, device_id=(i, z + 1), device_id_type=MESH)

    greeted = (1 + jnp.minimum(chip, hops) + jnp.minimum(n_loop // 2 - 1 - chip, hops)
               + jnp.minimum(z, 1) + jnp.minimum(n_tp - 1 - z, 1))
    pl.semaphore_wait(barrier, greeted)

    for d in range(1, hops + 1):
        @pl.when(i + 2 * d < n_loop)
        def _():
            id_chip(d).start()

    chip_each(lambda copy: copy.start())

    @pl.when(core == 0)
    def _():
        for copy in up_copies(0):
            copy.start()

    for k in range(1, reach + 1):
        @pl.when(i < k)
        def _():
            kv_buf[reach - k] = jnp.zeros(kv_buf.shape[1:], kv_buf.dtype)
            id_buf[reach - k] = jnp.full(id_buf.shape[1:], -1, id_buf.dtype)
    load_ids.wait()
    own_ids = id_buf[reach].astype(jnp.float32)
    square = (tok, tok)
    q_col[...] = jnp.max(
        jnp.where(lax.broadcasted_iota(jnp.int32, square, 0) == lax.broadcasted_iota(jnp.int32, square, 1),
                  jnp.broadcast_to(own_ids, square), -1.0), axis=1, keepdims=True)
    v_buf[:, HD:] = jnp.ones((v_buf.shape[0], HD), v_buf.dtype)
    load_kv.wait()
    load_q.wait()
    for d in range(hops, 0, -1):
        @pl.when(i >= 2 * d)
        def _():
            id_chip(d).wait_recv()
            kv_chip(0, d).wait_recv()
            kv_chip(1, d).wait_recv()

            @pl.when(core == 1)
            def _():
                for copy in down_copies(d):
                    copy.start()

            if d < hops:
                @pl.when(core == 0)
                def _():
                    for copy in up_copies(d):
                        copy.start()
    for d in range(1, hops + 1):
        @pl.when((core == 0) & (i >= 2 * d))
        def _():
            for copy in down_copies(d):
                copy.wait_recv()

        @pl.when((core == 1) & (i >= 2 * d - 1))
        def _():
            for copy in up_copies(d - 1):
                copy.wait_recv()
    for s in range(reach + 1):
        v_buf[s * tok:(s + 1) * tok, :HD] = kv_buf[s, :, HD:]

    def compute(b):
        rows = pl.ds(pl.multiple_of(b * ROWS, ROWS), ROWS)
        q_ids = q_col[rows, :]
        shape = (ROWS, tok)
        lower = (lax.broadcasted_iota(jnp.int32, shape, 1)
                 <= lax.broadcasted_iota(jnp.int32, shape, 0) + b * ROWS)
        key_ids = [jnp.broadcast_to(id_buf[s].astype(jnp.float32), shape) for s in range(reach + 1)]
        shared = jnp.where(lower, key_ids[reach], key_ids[0])
        for s, ids in enumerate([shared] + key_ids[1:reach]):
            bias[:, s * tok:(s + 1) * tok] = jnp.where(ids == q_ids, 0.0, BLOCKED)
        keys = kv_buf[:, :, :HD].reshape((reach + 1) * tok, HD)
        for h in range(0, heads, STACK):
            q = jnp.concatenate([q_ref[rows, (h + j) * HD:(h + j + 1) * HD] for j in range(STACK)], axis=0)
            s = lax.dot_general(q, keys, (((1,), (1,)), ((), ())), preferred_element_type=jnp.float32)
            s = s.reshape(STACK, ROWS, (reach + 1) * tok)
            s = jnp.concatenate(
                [jnp.where(lower[None], s[:, :, far_last:], s[:, :, :tok]), s[:, :, tok:far_last]], axis=2)
            s = s * scale + bias[...][None]
            p = jnp.exp2(s - jnp.max(s, axis=2, keepdims=True))
            first = p[:, :, :tok]
            p = jnp.concatenate(
                [jnp.where(lower[None], 0.0, first), p[:, :, tok:], jnp.where(lower[None], first, 0.0)], axis=2)
            p = p.reshape(STACK * ROWS, (reach + 1) * tok).astype(jnp.bfloat16)
            o = jnp.dot(p, v_buf[...], preferred_element_type=jnp.float32)
            o = (o[:, :HD] / o[:, HD:]).astype(jnp.bfloat16)
            for j in range(STACK):
                attn[:, (h + j) * HD:(h + j + 1) * HD] = o[j * ROWS:(j + 1) * ROWS]

        for j in range(n_tp):
            c = jnp.where(low_half, n_tp - 1 - j, j)

            @pl.when(b == 0)
            def _():
                load_w(j).wait()

            part[c, rows, :] = jnp.dot(
                attn[...], w_ref[:, pl.ds(pl.multiple_of(c * width, width), width)],
                preferred_element_type=jnp.float32).astype(jnp.bfloat16)

            @pl.when((z == 0) & (c >= 2))
            def _():
                right_copy(c, b).start()

            @pl.when((z == n_tp - 1) & (c < n_tp - 2))
            def _():
                left_copy(c, b).start()

        for n in range(given):
            @pl.when((b == n) & (chip == 2) & (z == 0))
            def _():
                side_first(1, n).start()

            @pl.when((b == n) & (chip == 2) & (z == n_tp - 1))
            def _():
                side_first(n_tp - 2, n).start()

    def forward_right(b):
        rows = pl.ds(pl.multiple_of(b * ROWS, ROWS), ROWS)
        for c in range(n_tp - 1, 1, -1):
            @pl.when(c > z)
            def _():
                copy = right_copy(c, b)
                copy.wait_recv()
                part[c, rows, :] = (part[c, rows, :].astype(jnp.float32)
                                    + recv_r[c, rows, :].astype(jnp.float32)).astype(jnp.bfloat16)
                copy.start()

    def forward_left(b):
        rows = pl.ds(pl.multiple_of(b * ROWS, ROWS), ROWS)
        for c in range(n_tp - 2):
            @pl.when(c < z)
            def _():
                copy = left_copy(c, b)
                copy.wait_recv()
                part[c, rows, :] = (part[c, rows, :].astype(jnp.float32)
                                    + recv_l[c, rows, :].astype(jnp.float32)).astype(jnp.bfloat16)
                copy.start()

    middle = jnp.logical_and(z > 0, z < n_tp - 1)

    def step(b, carry):
        @pl.when(b < blocks)
        def _():
            compute(b)

        right_b = b - jnp.where(low_half, 1, 2)
        left_b = b - jnp.where(low_half, 2, 1)

        @pl.when(middle & low_half & (right_b >= 0) & (right_b < blocks))
        def _():
            forward_right(right_b)

        @pl.when(middle & (left_b >= 0) & (left_b < blocks))
        def _():
            forward_left(left_b)

        @pl.when(middle & jnp.logical_not(low_half) & (right_b >= 0) & (right_b < blocks))
        def _():
            forward_right(right_b)
        return carry

    lax.fori_loop(0, blocks + 2, step, 0)

    def send_late(near, copy, step):
        for n in range(given):
            @pl.when(chip == 0)
            def _():
                side_first(near, n).wait_recv()
                side_second(step, n).start()

            @pl.when(chip != 2)
            def _():
                copy(near, n).start()
        for late in range(given, blocks):
            copy(near, late).start()

    @pl.when(z == 0)
    def _():
        for b in range(blocks):
            for c in range(n_tp - 1, 1, -1):
                right_copy(c, b).wait_send()
            if b == blocks - 2:
                send_late(1, right_copy, 1)

    @pl.when(z == n_tp - 1)
    def _():
        for b in range(blocks):
            for c in range(n_tp - 2):
                left_copy(c, b).wait_send()
            if b == blocks - 2:
                send_late(n_tp - 2, left_copy, -1)

    for n in range(given):
        @pl.when((chip == 0) & (z == 1))
        def _():
            side_second(1, n).wait_recv()
            side_third(1, recv_r, r_sem, n).start()

        @pl.when((chip == 0) & (z == n_tp - 2))
        def _():
            side_second(-1, n).wait_recv()
            side_third(n_tp - 2, recv_l, l_sem, n).start()

    def finish(n, carry):
        b = lax.rem(n + given, blocks)
        rows = pl.ds(pl.multiple_of(b * ROWS, ROWS), ROWS)

        @pl.when(z == 0)
        def _():
            left_copy(z, b).wait_recv()
            out_ref[rows, :] = (part[z, rows, :].astype(jnp.float32)
                                + recv_l[z, rows, :].astype(jnp.float32)).astype(out_ref.dtype)

        @pl.when(z == n_tp - 1)
        def _():
            right_copy(z, b).wait_recv()
            out_ref[rows, :] = (part[z, rows, :].astype(jnp.float32)
                                + recv_r[z, rows, :].astype(jnp.float32)).astype(out_ref.dtype)

        @pl.when(middle)
        def _():
            right_copy(z, b).wait_recv()
            left_copy(z, b).wait_recv()
            out_ref[rows, :] = (part[z, rows, :].astype(jnp.float32)
                                + recv_r[z, rows, :].astype(jnp.float32)
                                + recv_l[z, rows, :].astype(jnp.float32)).astype(out_ref.dtype)
        return carry

    lax.fori_loop(0, blocks, finish, 0)

    chip_each(lambda copy: copy.wait_send())
    for d in range(1, hops + 1):
        @pl.when(i + 2 * d < n_loop)
        def _():
            id_chip(d).wait_send()

        @pl.when((core == 1) & (i >= 2 * d))
        def _():
            for copy in down_copies(d):
                copy.wait_send()

        @pl.when((core == 0) & (i >= 2 * d - 2))
        def _():
            for copy in up_copies(d - 1):
                copy.wait_send()

    for n in range(given):
        @pl.when((chip == 2) & (z == 0))
        def _():
            side_first(1, n).wait_send()

        @pl.when((chip == 2) & (z == n_tp - 1))
        def _():
            side_first(n_tp - 2, n).wait_send()

        @pl.when((chip == 0) & (z == 0))
        def _():
            side_second(1, n).wait_send()

        @pl.when((chip == 0) & (z == n_tp - 1))
        def _():
            side_second(-1, n).wait_send()

        @pl.when((chip == 0) & (z == 1))
        def _():
            side_third(1, recv_r, r_sem, n).wait_send()

        @pl.when((chip == 0) & (z == n_tp - 2))
        def _():
            side_third(n_tp - 2, recv_l, l_sem, n).wait_send()

    def drain(b, carry):
        direct = (b >= given) | (chip != 2)

        @pl.when((z == 0) & direct)
        def _():
            right_copy(1, b).wait_send()

        @pl.when((z == n_tp - 1) & direct)
        def _():
            left_copy(n_tp - 2, b).wait_send()

        for c in range(n_tp):
            @pl.when(middle & (c > z))
            def _():
                right_copy(c, b).wait_send()

            @pl.when(middle & (c < z))
            def _():
                left_copy(c, b).wait_send()
        return carry

    lax.fori_loop(0, blocks, drain, 0)


def per_device(queries, key_values, prompt_ids, out_weight):
    n_loop, n_tp = lax.axis_size("loop"), lax.axis_size("tp")
    tok, q_cols = queries.shape
    depth, d_out = out_weight.shape
    width = d_out // n_tp
    reach = min(8, n_loop // 2)
    blocks = tok // ROWS
    hops = reach // 2
    vmem = pltpu.VMEM
    dma = pltpu.SemaphoreType.DMA
    any_spec = pl.BlockSpec(memory_space=pl.ANY)
    vmem_spec = pl.BlockSpec(memory_space=pltpu.VMEM)
    return pl.pallas_call(
        functools.partial(kernel, n_loop, n_tp, reach),
        out_shape=pltpu.VMEM((tok, width), jnp.bfloat16),
        in_specs=[any_spec] * 4,
        out_specs=vmem_spec,
        scratch_shapes=[
            vmem((tok, q_cols), jnp.bfloat16),
            vmem((reach + 1, tok, 2 * HD), jnp.bfloat16),
            vmem(((reach + 1) * tok, 2 * HD), jnp.bfloat16),
            vmem((reach + 1, 1, tok), jnp.int32),
            vmem((tok, 1), jnp.float32),
            vmem((ROWS, reach * tok), jnp.float32),
            vmem((ROWS, q_cols), jnp.bfloat16),
            vmem((depth, d_out), jnp.bfloat16),
            vmem((n_tp, tok, width), jnp.bfloat16),
            vmem((n_tp, tok, width), jnp.bfloat16),
            vmem((n_tp, tok, width), jnp.bfloat16),
            vmem((2, ROWS, width), jnp.bfloat16),
            vmem((2, ROWS, width), jnp.bfloat16),
            dma((3,)), dma((n_tp,)), dma((reach,)), dma((reach,)), dma((2, hops)), dma((2, hops)), dma((5, 2)),
            dma((reach,)), dma((reach,)),
            dma((n_tp, blocks)), dma((n_tp, blocks)), dma((n_tp, blocks)),
        ],
        compiler_params=pltpu.CompilerParams(
            collective_id=0, has_side_effects=True, vmem_limit_bytes=32 * 1024 * 1024),
        cost_estimate=pl.CostEstimate(flops=3_500_000_000, bytes_accessed=10_000_000, transcendentals=2_000_000),
    )(*(pltpu.with_memory_space_constraint(x, pltpu.HBM)
        for x in (queries, key_values, prompt_ids.reshape(1, tok), out_weight)))


def solution(mesh):
    in_specs = (P("loop", "tp"), P("loop", "tp"), P("loop"), P("tp", None))
    out_specs = P("loop", "tp")
    return jax.shard_map(
        per_device, mesh=mesh, in_specs=in_specs, out_specs=out_specs, check_vma=False
    )
```

```python
import functools
import math

import jax
import jax.numpy as jnp
from jax import lax
from jax.experimental import pallas as pl
from jax.experimental.pallas import tpu as pltpu
from jax.sharding import PartitionSpec as P

HD = 128
BLOCKED = -1e30
ROWS = 32
STACK = 4
MESH = pl.DeviceIdType.MESH


def kernel(n_loop, n_tp, reach, q_hbm, kv_hbm, ids_hbm, w_hbm, out_ref,
           q_ref, kv_buf, v_buf, id_buf, q_col, bias, attn, w_ref, part, recv_r, recv_l, side_a, side_b,
           load_sem, w_sem, kv_send, kv_recv, chip_send, chip_recv, side_sem, id_send, id_recv, send_sem, r_sem, l_sem):
    tok = q_ref.shape[0]
    heads = q_ref.shape[1] // HD
    width = part.shape[2]
    blocks = tok // ROWS
    far_last = reach * tok
    scale = math.log2(math.e) / math.sqrt(HD)
    i = lax.axis_index("loop")
    z = lax.axis_index("tp")

    load_q = pltpu.make_async_copy(q_hbm, q_ref, load_sem.at[0])
    load_kv = pltpu.make_async_copy(kv_hbm, kv_buf.at[reach], load_sem.at[1])
    low_half = z < n_tp // 2

    def load_w(j):
        c = jnp.where(low_half, n_tp - 1 - j, j)
        cols = pl.ds(pl.multiple_of(c * width, width), width)
        return pltpu.make_async_copy(w_hbm.at[:, cols], w_ref.at[:, cols], w_sem.at[j])

    load_ids = pltpu.make_async_copy(ids_hbm, id_buf.at[reach], load_sem.at[2])

    core = lax.rem(i, 2)
    chip = i // 2
    hops = reach // 2

    half = tok // 2

    def id_chip(d):
        return pltpu.make_async_remote_copy(
            src_ref=ids_hbm, dst_ref=id_buf.at[reach - 2 * d], send_sem=id_send.at[d - 1],
            recv_sem=id_recv.at[2 * d - 1], device_id=(i + 2 * d, z), device_id_type=MESH)

    def kv_chip(h, d):
        rows = pl.ds(h * half, half)
        return pltpu.make_async_remote_copy(
            src_ref=kv_hbm.at[rows], dst_ref=kv_buf.at[reach - 2 * d, rows],
            send_sem=chip_send.at[h, d - 1], recv_sem=chip_recv.at[h, d - 1],
            device_id=(i + 2 * d, z), device_id_type=MESH)

    def chip_each(act):
        for h in range(2):
            for d in range(hops, 0, -1):
                @pl.when(i + 2 * d < n_loop)
                def _():
                    act(kv_chip(h, d))

    def up_copies(d):
        return [
            pltpu.make_async_remote_copy(
                src_ref=source if d == 0 else target.at[reach - 2 * d], dst_ref=target.at[reach - 2 * d - 1],
                send_sem=sends.at[hops + d], recv_sem=arrivals.at[2 * d],
                device_id=(i + 1, z), device_id_type=MESH)
            for source, target, sends, arrivals in (
                (ids_hbm, id_buf, id_send, id_recv), (kv_hbm, kv_buf, kv_send, kv_recv))]

    def down_copies(d):
        return [
            pltpu.make_async_remote_copy(
                src_ref=target.at[reach - 2 * d], dst_ref=target.at[reach - 2 * d + 1],
                send_sem=sends.at[hops + d - 1], recv_sem=arrivals.at[2 * d - 2],
                device_id=(i - 1, z), device_id_type=MESH)
            for target, sends, arrivals in ((id_buf, id_send, id_recv), (kv_buf, kv_send, kv_recv))]

    def right_copy(c, b):
        rows = pl.ds(pl.multiple_of(b * ROWS, ROWS), ROWS)
        return pltpu.make_async_remote_copy(
            src_ref=part.at[c, rows], dst_ref=recv_r.at[c, rows], send_sem=send_sem.at[c, b],
            recv_sem=r_sem.at[c, b], device_id=(i, z + 1), device_id_type=MESH)

    def left_copy(c, b):
        rows = pl.ds(pl.multiple_of(b * ROWS, ROWS), ROWS)
        return pltpu.make_async_remote_copy(
            src_ref=part.at[c, rows], dst_ref=recv_l.at[c, rows], send_sem=send_sem.at[c, b],
            recv_sem=l_sem.at[c, b], device_id=(i, z - 1), device_id_type=MESH)

    side = n_loop == 8 and n_tp >= 4 and reach == 4
    given = 2 if side else 0

    def side_first(c, b):
        return pltpu.make_async_remote_copy(
            src_ref=part.at[c, pl.ds(b * ROWS, ROWS)], dst_ref=side_a.at[b], send_sem=side_sem.at[0, b],
            recv_sem=side_sem.at[1, b], device_id=(i - 4, z), device_id_type=MESH)

    def side_second(step, b):
        return pltpu.make_async_remote_copy(
            src_ref=side_a.at[b], dst_ref=side_b.at[b], send_sem=side_sem.at[2, b],
            recv_sem=side_sem.at[3, b], device_id=(i, z + step), device_id_type=MESH)

    def side_third(c, target, sems, b):
        return pltpu.make_async_remote_copy(
            src_ref=side_b.at[b], dst_ref=target.at[c, pl.ds(b * ROWS, ROWS)], send_sem=side_sem.at[4, b],
            recv_sem=sems.at[c, b], device_id=(i + 4, z), device_id_type=MESH)

    barrier = pltpu.get_barrier_semaphore()
    pl.semaphore_signal(barrier, inc=1, device_id=(i + 1 - 2 * core, z), device_id_type=MESH)
    for d in range(1, hops + 1):
        @pl.when(i + 2 * d < n_loop)
        def _():
            pl.semaphore_signal(barrier, inc=1, device_id=(i + 2 * d, z), device_id_type=MESH)

        @pl.when(i - 2 * d >= 0)
        def _():
            pl.semaphore_signal(barrier, inc=1, device_id=(i - 2 * d, z), device_id_type=MESH)

    @pl.when(z > 0)
    def _():
        pl.semaphore_signal(barrier, inc=1, device_id=(i, z - 1), device_id_type=MESH)

    @pl.when(z < n_tp - 1)
    def _():
        pl.semaphore_signal(barrier, inc=1, device_id=(i, z + 1), device_id_type=MESH)

    greeted = (1 + jnp.minimum(chip, hops) + jnp.minimum(n_loop // 2 - 1 - chip, hops)
               + jnp.minimum(z, 1) + jnp.minimum(n_tp - 1 - z, 1))
    load_ids.start()
    load_kv.start()
    load_q.start()
    for j in range(n_tp):
        load_w(j).start()
    pl.semaphore_wait(barrier, greeted)

    for d in range(1, hops + 1):
        @pl.when(i + 2 * d < n_loop)
        def _():
            id_chip(d).start()

    chip_each(lambda copy: copy.start())

    @pl.when(core == 0)
    def _():
        for copy in up_copies(0):
            copy.start()

    for k in range(1, reach + 1):
        @pl.when(i < k)
        def _():
            kv_buf[reach - k] = jnp.zeros(kv_buf.shape[1:], kv_buf.dtype)
            id_buf[reach - k] = jnp.full(id_buf.shape[1:], -1, id_buf.dtype)
    load_ids.wait()
    own_ids = id_buf[reach].astype(jnp.float32)
    square = (tok, tok)
    q_col[...] = jnp.max(
        jnp.where(lax.broadcasted_iota(jnp.int32, square, 0) == lax.broadcasted_iota(jnp.int32, square, 1),
                  jnp.broadcast_to(own_ids, square), -1.0), axis=1, keepdims=True)
    v_buf[:, HD:] = jnp.ones((v_buf.shape[0], HD), v_buf.dtype)
    load_kv.wait()
    load_q.wait()
    for d in range(hops, 0, -1):
        @pl.when(i >= 2 * d)
        def _():
            id_chip(d).wait_recv()
            kv_chip(0, d).wait_recv()
            kv_chip(1, d).wait_recv()

            @pl.when(core == 1)
            def _():
                for copy in down_copies(d):
                    copy.start()

            if d < hops:
                @pl.when(core == 0)
                def _():
                    for copy in up_copies(d):
                        copy.start()
    for d in range(1, hops + 1):
        @pl.when((core == 0) & (i >= 2 * d))
        def _():
            for copy in down_copies(d):
                copy.wait_recv()

        @pl.when((core == 1) & (i >= 2 * d - 1))
        def _():
            for copy in up_copies(d - 1):
                copy.wait_recv()
    for s in range(reach + 1):
        v_buf[s * tok:(s + 1) * tok, :HD] = kv_buf[s, :, HD:]

    def compute(b):
        rows = pl.ds(pl.multiple_of(b * ROWS, ROWS), ROWS)
        q_ids = q_col[rows, :]
        shape = (ROWS, tok)
        lower = (lax.broadcasted_iota(jnp.int32, shape, 1)
                 <= lax.broadcasted_iota(jnp.int32, shape, 0) + b * ROWS)
        key_ids = [jnp.broadcast_to(id_buf[s].astype(jnp.float32), shape) for s in range(reach + 1)]
        shared = jnp.where(lower, key_ids[reach], key_ids[0])
        for s, ids in enumerate([shared] + key_ids[1:reach]):
            bias[:, s * tok:(s + 1) * tok] = jnp.where(ids == q_ids, 0.0, BLOCKED)
        keys = kv_buf[:, :, :HD].reshape((reach + 1) * tok, HD)
        for h in range(0, heads, STACK):
            q = jnp.concatenate([q_ref[rows, (h + j) * HD:(h + j + 1) * HD] for j in range(STACK)], axis=0)
            s = lax.dot_general(q, keys, (((1,), (1,)), ((), ())), preferred_element_type=jnp.float32)
            s = s.reshape(STACK, ROWS, (reach + 1) * tok)
            s = jnp.concatenate(
                [jnp.where(lower[None], s[:, :, far_last:], s[:, :, :tok]), s[:, :, tok:far_last]], axis=2)
            s = s * scale + bias[...][None]
            p = jnp.exp2(s - jnp.max(s, axis=2, keepdims=True))
            first = p[:, :, :tok]
            p = jnp.concatenate(
                [jnp.where(lower[None], 0.0, first), p[:, :, tok:], jnp.where(lower[None], first, 0.0)], axis=2)
            p = p.reshape(STACK * ROWS, (reach + 1) * tok).astype(jnp.bfloat16)
            o = jnp.dot(p, v_buf[...], preferred_element_type=jnp.float32)
            o = (o[:, :HD] / o[:, HD:]).astype(jnp.bfloat16)
            for j in range(STACK):
                attn[:, (h + j) * HD:(h + j + 1) * HD] = o[j * ROWS:(j + 1) * ROWS]

        for j in range(n_tp):
            c = jnp.where(low_half, n_tp - 1 - j, j)

            @pl.when(b == 0)
            def _():
                load_w(j).wait()

            part[c, rows, :] = jnp.dot(
                attn[...], w_ref[:, pl.ds(pl.multiple_of(c * width, width), width)],
                preferred_element_type=jnp.float32).astype(jnp.bfloat16)

            @pl.when((z == 0) & (c >= 2))
            def _():
                right_copy(c, b).start()

            @pl.when((z == n_tp - 1) & (c < n_tp - 2))
            def _():
                left_copy(c, b).start()

        for n in range(given):
            @pl.when((b == n) & (chip == 2) & (z == 0))
            def _():
                side_first(1, n).start()

            @pl.when((b == n) & (chip == 2) & (z == n_tp - 1))
            def _():
                side_first(n_tp - 2, n).start()

    def forward_right(b):
        rows = pl.ds(pl.multiple_of(b * ROWS, ROWS), ROWS)
        for c in range(n_tp - 1, 1, -1):
            @pl.when(c > z)
            def _():
                copy = right_copy(c, b)
                copy.wait_recv()
                part[c, rows, :] = (part[c, rows, :].astype(jnp.float32)
                                    + recv_r[c, rows, :].astype(jnp.float32)).astype(jnp.bfloat16)
                copy.start()

    def forward_left(b):
        rows = pl.ds(pl.multiple_of(b * ROWS, ROWS), ROWS)
        for c in range(n_tp - 2):
            @pl.when(c < z)
            def _():
                copy = left_copy(c, b)
                copy.wait_recv()
                part[c, rows, :] = (part[c, rows, :].astype(jnp.float32)
                                    + recv_l[c, rows, :].astype(jnp.float32)).astype(jnp.bfloat16)
                copy.start()

    middle = jnp.logical_and(z > 0, z < n_tp - 1)

    def step(b, carry):
        @pl.when(b < blocks)
        def _():
            compute(b)

        right_b = b - jnp.where(low_half, 1, 2)
        left_b = b - jnp.where(low_half, 2, 1)

        @pl.when(middle & low_half & (right_b >= 0) & (right_b < blocks))
        def _():
            forward_right(right_b)

        @pl.when(middle & (left_b >= 0) & (left_b < blocks))
        def _():
            forward_left(left_b)

        @pl.when(middle & jnp.logical_not(low_half) & (right_b >= 0) & (right_b < blocks))
        def _():
            forward_right(right_b)
        return carry

    lax.fori_loop(0, blocks + 2, step, 0)

    def send_late(near, copy, step):
        for n in range(given):
            @pl.when(chip == 0)
            def _():
                side_first(near, n).wait_recv()
                side_second(step, n).start()

            @pl.when(chip != 2)
            def _():
                copy(near, n).start()
        for late in range(given, blocks):
            copy(near, late).start()

    @pl.when(z == 0)
    def _():
        for b in range(blocks):
            for c in range(n_tp - 1, 1, -1):
                right_copy(c, b).wait_send()
            if b == blocks - 2:
                send_late(1, right_copy, 1)

    @pl.when(z == n_tp - 1)
    def _():
        for b in range(blocks):
            for c in range(n_tp - 2):
                left_copy(c, b).wait_send()
            if b == blocks - 2:
                send_late(n_tp - 2, left_copy, -1)

    for n in range(given):
        @pl.when((chip == 0) & (z == 1))
        def _():
            side_second(1, n).wait_recv()
            side_third(1, recv_r, r_sem, n).start()

        @pl.when((chip == 0) & (z == n_tp - 2))
        def _():
            side_second(-1, n).wait_recv()
            side_third(n_tp - 2, recv_l, l_sem, n).start()

    chip_each(lambda copy: copy.wait_send())
    for d in range(1, hops + 1):
        @pl.when(i + 2 * d < n_loop)
        def _():
            id_chip(d).wait_send()

        @pl.when((core == 1) & (i >= 2 * d))
        def _():
            for copy in down_copies(d):
                copy.wait_send()

        @pl.when((core == 0) & (i >= 2 * d - 2))
        def _():
            for copy in up_copies(d - 1):
                copy.wait_send()

    for n in range(given):
        @pl.when((chip == 2) & (z == 0))
        def _():
            side_first(1, n).wait_send()

        @pl.when((chip == 2) & (z == n_tp - 1))
        def _():
            side_first(n_tp - 2, n).wait_send()

    def drain(b, carry):
        for c in range(n_tp):
            @pl.when(middle & (c > z))
            def _():
                right_copy(c, b).wait_send()

            @pl.when(middle & (c < z))
            def _():
                left_copy(c, b).wait_send()
        return carry

    lax.fori_loop(0, blocks, drain, 0)

    def finish(n, carry):
        b = lax.rem(n + given, blocks)
        rows = pl.ds(pl.multiple_of(b * ROWS, ROWS), ROWS)

        @pl.when(z == 0)
        def _():
            left_copy(z, b).wait_recv()
            out_ref[rows, :] = (part[z, rows, :].astype(jnp.float32)
                                + recv_l[z, rows, :].astype(jnp.float32)).astype(out_ref.dtype)

        @pl.when(z == n_tp - 1)
        def _():
            right_copy(z, b).wait_recv()
            out_ref[rows, :] = (part[z, rows, :].astype(jnp.float32)
                                + recv_r[z, rows, :].astype(jnp.float32)).astype(out_ref.dtype)

        @pl.when(middle)
        def _():
            right_copy(z, b).wait_recv()
            left_copy(z, b).wait_recv()
            out_ref[rows, :] = (part[z, rows, :].astype(jnp.float32)
                                + recv_r[z, rows, :].astype(jnp.float32)
                                + recv_l[z, rows, :].astype(jnp.float32)).astype(out_ref.dtype)
        return carry

    lax.fori_loop(0, blocks, finish, 0)

    def drain_late(b, carry):
        direct = (b >= given) | (chip != 2)

        @pl.when((z == 0) & direct)
        def _():
            right_copy(1, b).wait_send()

        @pl.when((z == n_tp - 1) & direct)
        def _():
            left_copy(n_tp - 2, b).wait_send()
        return carry

    lax.fori_loop(0, blocks, drain_late, 0)
    for n in range(given):
        @pl.when((chip == 0) & (z == 0))
        def _():
            side_second(1, n).wait_send()

        @pl.when((chip == 0) & (z == n_tp - 1))
        def _():
            side_second(-1, n).wait_send()

        @pl.when((chip == 0) & (z == 1))
        def _():
            side_third(1, recv_r, r_sem, n).wait_send()

        @pl.when((chip == 0) & (z == n_tp - 2))
        def _():
            side_third(n_tp - 2, recv_l, l_sem, n).wait_send()


def per_device(queries, key_values, prompt_ids, out_weight):
    n_loop, n_tp = lax.axis_size("loop"), lax.axis_size("tp")
    tok, q_cols = queries.shape
    depth, d_out = out_weight.shape
    width = d_out // n_tp
    reach = min(8, n_loop // 2)
    blocks = tok // ROWS
    hops = reach // 2
    vmem = pltpu.VMEM
    dma = pltpu.SemaphoreType.DMA
    any_spec = pl.BlockSpec(memory_space=pl.ANY)
    vmem_spec = pl.BlockSpec(memory_space=pltpu.VMEM)
    return pl.pallas_call(
        functools.partial(kernel, n_loop, n_tp, reach),
        out_shape=pltpu.VMEM((tok, width), jnp.bfloat16),
        in_specs=[any_spec] * 4,
        out_specs=vmem_spec,
        scratch_shapes=[
            vmem((tok, q_cols), jnp.bfloat16),
            vmem((reach + 1, tok, 2 * HD), jnp.bfloat16),
            vmem(((reach + 1) * tok, 2 * HD), jnp.bfloat16),
            vmem((reach + 1, 1, tok), jnp.int32),
            vmem((tok, 1), jnp.float32),
            vmem((ROWS, reach * tok), jnp.float32),
            vmem((ROWS, q_cols), jnp.bfloat16),
            vmem((depth, d_out), jnp.bfloat16),
            vmem((n_tp, tok, width), jnp.bfloat16),
            vmem((n_tp, tok, width), jnp.bfloat16),
            vmem((n_tp, tok, width), jnp.bfloat16),
            vmem((2, ROWS, width), jnp.bfloat16),
            vmem((2, ROWS, width), jnp.bfloat16),
            dma((3,)), dma((n_tp,)), dma((reach,)), dma((reach,)), dma((2, hops)), dma((2, hops)), dma((5, 2)),
            dma((reach,)), dma((reach,)),
            dma((n_tp, blocks)), dma((n_tp, blocks)), dma((n_tp, blocks)),
        ],
        compiler_params=pltpu.CompilerParams(
            collective_id=0, has_side_effects=True, vmem_limit_bytes=32 * 1024 * 1024),
        cost_estimate=pl.CostEstimate(flops=3_500_000_000, bytes_accessed=10_000_000, transcendentals=2_000_000),
    )(*(pltpu.with_memory_space_constraint(x, pltpu.HBM)
        for x in (queries, key_values, prompt_ids.reshape(1, tok), out_weight)))


def solution(mesh):
    in_specs = (P("loop", "tp"), P("loop", "tp"), P("loop"), P("tp", None))
    out_specs = P("loop", "tp")
    return jax.shard_map(
        per_device, mesh=mesh, in_specs=in_specs, out_specs=out_specs, check_vma=False
    )
```

```python
import functools
import math

import jax
import jax.numpy as jnp
from jax import lax
from jax.experimental import pallas as pl
from jax.experimental.pallas import tpu as pltpu
from jax.sharding import PartitionSpec as P

HD = 128
BLOCKED = -1e30
ROWS = 32
STACK = 4
MESH = pl.DeviceIdType.MESH


def kernel(n_loop, n_tp, reach, q_hbm, kv_hbm, ids_hbm, w_hbm, out_ref,
           q_ref, kv_buf, v_buf, id_buf, q_col, bias, attn, w_ref, part, recv_r, recv_l, side_a, side_b,
           load_sem, w_sem, kv_send, kv_recv, chip_send, chip_recv, side_sem, id_send, id_recv, send_sem, r_sem, l_sem):
    tok = q_ref.shape[0]
    heads = q_ref.shape[1] // HD
    width = part.shape[2]
    blocks = tok // ROWS
    far_last = reach * tok
    scale = math.log2(math.e) / math.sqrt(HD)
    i = lax.axis_index("loop")
    z = lax.axis_index("tp")

    load_q = pltpu.make_async_copy(q_hbm, q_ref, load_sem.at[0])
    load_kv = pltpu.make_async_copy(kv_hbm, kv_buf.at[reach], load_sem.at[1])
    low_half = z < n_tp // 2

    def load_w(j):
        c = jnp.where(low_half, n_tp - 1 - j, j)
        cols = pl.ds(pl.multiple_of(c * width, width), width)
        return pltpu.make_async_copy(w_hbm.at[:, cols], w_ref.at[:, cols], w_sem.at[j])

    load_ids = pltpu.make_async_copy(ids_hbm, id_buf.at[reach], load_sem.at[2])

    core = lax.rem(i, 2)
    chip = i // 2
    hops = reach // 2

    half = tok // 2

    def id_chip(d):
        return pltpu.make_async_remote_copy(
            src_ref=ids_hbm, dst_ref=id_buf.at[reach - 2 * d], send_sem=id_send.at[d - 1],
            recv_sem=id_recv.at[2 * d - 1], device_id=(i + 2 * d, z), device_id_type=MESH)

    def kv_chip(h, d):
        rows = pl.ds(h * half, half)
        return pltpu.make_async_remote_copy(
            src_ref=kv_hbm.at[rows], dst_ref=kv_buf.at[reach - 2 * d, rows],
            send_sem=chip_send.at[h, d - 1], recv_sem=chip_recv.at[h, d - 1],
            device_id=(i + 2 * d, z), device_id_type=MESH)

    def chip_each(act):
        for h in range(2):
            for d in range(hops, 0, -1):
                @pl.when(i + 2 * d < n_loop)
                def _():
                    act(kv_chip(h, d))

    def up_copies(d):
        return [
            pltpu.make_async_remote_copy(
                src_ref=source if d == 0 else target.at[reach - 2 * d], dst_ref=target.at[reach - 2 * d - 1],
                send_sem=sends.at[hops + d], recv_sem=arrivals.at[2 * d],
                device_id=(i + 1, z), device_id_type=MESH)
            for source, target, sends, arrivals in (
                (ids_hbm, id_buf, id_send, id_recv), (kv_hbm, kv_buf, kv_send, kv_recv))]

    def down_copies(d):
        return [
            pltpu.make_async_remote_copy(
                src_ref=target.at[reach - 2 * d], dst_ref=target.at[reach - 2 * d + 1],
                send_sem=sends.at[hops + d - 1], recv_sem=arrivals.at[2 * d - 2],
                device_id=(i - 1, z), device_id_type=MESH)
            for target, sends, arrivals in ((id_buf, id_send, id_recv), (kv_buf, kv_send, kv_recv))]

    def right_copy(c, b):
        rows = pl.ds(pl.multiple_of(b * ROWS, ROWS), ROWS)
        return pltpu.make_async_remote_copy(
            src_ref=part.at[c, rows], dst_ref=recv_r.at[c, rows], send_sem=send_sem.at[c, b],
            recv_sem=r_sem.at[c, b], device_id=(i, z + 1), device_id_type=MESH)

    def left_copy(c, b):
        rows = pl.ds(pl.multiple_of(b * ROWS, ROWS), ROWS)
        return pltpu.make_async_remote_copy(
            src_ref=part.at[c, rows], dst_ref=recv_l.at[c, rows], send_sem=send_sem.at[c, b],
            recv_sem=l_sem.at[c, b], device_id=(i, z - 1), device_id_type=MESH)

    side = n_loop == 8 and n_tp >= 4 and reach == 4
    given = 2 if side else 0

    def side_first(c, b):
        return pltpu.make_async_remote_copy(
            src_ref=part.at[c, pl.ds(b * ROWS, ROWS)], dst_ref=side_a.at[b], send_sem=side_sem.at[0, b],
            recv_sem=side_sem.at[1, b], device_id=(i - 4, z), device_id_type=MESH)

    def side_second(step, b):
        return pltpu.make_async_remote_copy(
            src_ref=side_a.at[b], dst_ref=side_b.at[b], send_sem=side_sem.at[2, b],
            recv_sem=side_sem.at[3, b], device_id=(i, z + step), device_id_type=MESH)

    def side_third(c, target, sems, b):
        return pltpu.make_async_remote_copy(
            src_ref=side_b.at[b], dst_ref=target.at[c, pl.ds(b * ROWS, ROWS)], send_sem=side_sem.at[4, b],
            recv_sem=sems.at[c, b], device_id=(i + 4, z), device_id_type=MESH)

    barrier = pltpu.get_barrier_semaphore()
    pl.semaphore_signal(barrier, inc=1, device_id=(i + 1 - 2 * core, z), device_id_type=MESH)
    for d in range(1, hops + 1):
        @pl.when(i + 2 * d < n_loop)
        def _():
            pl.semaphore_signal(barrier, inc=1, device_id=(i + 2 * d, z), device_id_type=MESH)

        @pl.when(i - 2 * d >= 0)
        def _():
            pl.semaphore_signal(barrier, inc=1, device_id=(i - 2 * d, z), device_id_type=MESH)

    @pl.when(z > 0)
    def _():
        pl.semaphore_signal(barrier, inc=1, device_id=(i, z - 1), device_id_type=MESH)

    @pl.when(z < n_tp - 1)
    def _():
        pl.semaphore_signal(barrier, inc=1, device_id=(i, z + 1), device_id_type=MESH)

    greeted = (1 + jnp.minimum(chip, hops) + jnp.minimum(n_loop // 2 - 1 - chip, hops)
               + jnp.minimum(z, 1) + jnp.minimum(n_tp - 1 - z, 1))
    load_ids.start()
    load_kv.start()
    load_q.start()
    for j in range(n_tp):
        load_w(j).start()
    pl.semaphore_wait(barrier, greeted)

    for d in range(1, hops + 1):
        @pl.when(i + 2 * d < n_loop)
        def _():
            id_chip(d).start()

    chip_each(lambda copy: copy.start())

    @pl.when(core == 0)
    def _():
        for copy in up_copies(0):
            copy.start()

    for k in range(1, reach + 1):
        @pl.when(i < k)
        def _():
            kv_buf[reach - k] = jnp.zeros(kv_buf.shape[1:], kv_buf.dtype)
            id_buf[reach - k] = jnp.full(id_buf.shape[1:], -1, id_buf.dtype)
    load_ids.wait()
    own_ids = id_buf[reach].astype(jnp.float32)
    square = (tok, tok)
    q_col[...] = jnp.max(
        jnp.where(lax.broadcasted_iota(jnp.int32, square, 0) == lax.broadcasted_iota(jnp.int32, square, 1),
                  jnp.broadcast_to(own_ids, square), -1.0), axis=1, keepdims=True)
    v_buf[:, HD:] = jnp.ones((v_buf.shape[0], HD), v_buf.dtype)
    load_kv.wait()
    load_q.wait()
    for d in range(hops, 0, -1):
        @pl.when(i >= 2 * d)
        def _():
            id_chip(d).wait_recv()
            kv_chip(0, d).wait_recv()
            kv_chip(1, d).wait_recv()

            @pl.when(core == 1)
            def _():
                for copy in down_copies(d):
                    copy.start()

            if d < hops:
                @pl.when(core == 0)
                def _():
                    for copy in up_copies(d):
                        copy.start()
    for d in range(1, hops + 1):
        @pl.when((core == 0) & (i >= 2 * d))
        def _():
            for copy in down_copies(d):
                copy.wait_recv()

        @pl.when((core == 1) & (i >= 2 * d - 1))
        def _():
            for copy in up_copies(d - 1):
                copy.wait_recv()
    for s in range(reach + 1):
        v_buf[s * tok:(s + 1) * tok, :HD] = kv_buf[s, :, HD:]

    def compute(b):
        rows = pl.ds(pl.multiple_of(b * ROWS, ROWS), ROWS)
        q_ids = q_col[rows, :]
        shape = (ROWS, tok)
        lower = (lax.broadcasted_iota(jnp.int32, shape, 1)
                 <= lax.broadcasted_iota(jnp.int32, shape, 0) + b * ROWS)
        key_ids = [jnp.broadcast_to(id_buf[s].astype(jnp.float32), shape) for s in range(reach + 1)]
        shared = jnp.where(lower, key_ids[reach], key_ids[0])
        for s, ids in enumerate([shared] + key_ids[1:reach]):
            bias[:, s * tok:(s + 1) * tok] = jnp.where(ids == q_ids, 0.0, BLOCKED)
        keys = kv_buf[:, :, :HD].reshape((reach + 1) * tok, HD)
        for h in range(0, heads, STACK):
            q = jnp.concatenate([q_ref[rows, (h + j) * HD:(h + j + 1) * HD] for j in range(STACK)], axis=0)
            s = lax.dot_general(q, keys, (((1,), (1,)), ((), ())), preferred_element_type=jnp.float32)
            s = s.reshape(STACK, ROWS, (reach + 1) * tok)
            s = jnp.concatenate(
                [jnp.where(lower[None], s[:, :, far_last:], s[:, :, :tok]), s[:, :, tok:far_last]], axis=2)
            s = s * scale + bias[...][None]
            p = jnp.exp2(s - jnp.max(s, axis=2, keepdims=True))
            first = p[:, :, :tok]
            p = jnp.concatenate(
                [jnp.where(lower[None], 0.0, first), p[:, :, tok:], jnp.where(lower[None], first, 0.0)], axis=2)
            p = p.reshape(STACK * ROWS, (reach + 1) * tok).astype(jnp.bfloat16)
            o = jnp.dot(p, v_buf[...], preferred_element_type=jnp.float32)
            o = (o[:, :HD] / o[:, HD:]).astype(jnp.bfloat16)
            for j in range(STACK):
                attn[:, (h + j) * HD:(h + j + 1) * HD] = o[j * ROWS:(j + 1) * ROWS]

        for j in range(n_tp):
            c = jnp.where(low_half, n_tp - 1 - j, j)

            @pl.when(b == 0)
            def _():
                load_w(j).wait()

            part[c, rows, :] = jnp.dot(
                attn[...], w_ref[:, pl.ds(pl.multiple_of(c * width, width), width)],
                preferred_element_type=jnp.float32).astype(jnp.bfloat16)

            @pl.when((z == 0) & (c >= 2))
            def _():
                right_copy(c, b).start()

            @pl.when((z == n_tp - 1) & (c < n_tp - 2))
            def _():
                left_copy(c, b).start()

        for n in range(given):
            @pl.when((b == n) & (chip == 2) & (z == 0))
            def _():
                side_first(1, n).start()

            @pl.when((b == n) & (chip == 2) & (z == n_tp - 1))
            def _():
                side_first(n_tp - 2, n).start()

    def forward_right(b):
        rows = pl.ds(pl.multiple_of(b * ROWS, ROWS), ROWS)
        for c in range(n_tp - 1, 1, -1):
            @pl.when(c > z)
            def _():
                copy = right_copy(c, b)
                copy.wait_recv()
                part[c, rows, :] = (part[c, rows, :].astype(jnp.float32)
                                    + recv_r[c, rows, :].astype(jnp.float32)).astype(jnp.bfloat16)
                copy.start()

    def forward_left(b):
        rows = pl.ds(pl.multiple_of(b * ROWS, ROWS), ROWS)
        for c in range(n_tp - 2):
            @pl.when(c < z)
            def _():
                copy = left_copy(c, b)
                copy.wait_recv()
                part[c, rows, :] = (part[c, rows, :].astype(jnp.float32)
                                    + recv_l[c, rows, :].astype(jnp.float32)).astype(jnp.bfloat16)
                copy.start()

    middle = jnp.logical_and(z > 0, z < n_tp - 1)

    def step(b, carry):
        @pl.when(b < blocks)
        def _():
            compute(b)

        right_b = b - jnp.where(low_half, 1, 2)
        left_b = b - jnp.where(low_half, 2, 1)

        @pl.when(middle & low_half & (right_b >= 0) & (right_b < blocks))
        def _():
            forward_right(right_b)

        @pl.when(middle & (left_b >= 0) & (left_b < blocks))
        def _():
            forward_left(left_b)

        @pl.when(middle & jnp.logical_not(low_half) & (right_b >= 0) & (right_b < blocks))
        def _():
            forward_right(right_b)
        return carry

    lax.fori_loop(0, blocks + 2, step, 0)

    def send_some(near, copy, step):
        if not given:
            copy(near, 0).start()
            return

        @pl.when(chip == 0)
        def _():
            for n in range(given):
                side_first(near, n).wait_recv()
                side_second(step, n).start()

        @pl.when(chip == 2)
        def _():
            copy(near, given).start()

        @pl.when(chip != 2)
        def _():
            copy(near, 0).start()

    def send_rest(near, copy):
        for late in range(1, blocks):
            if 0 < late <= given:
                @pl.when(chip != 2)
                def _():
                    copy(near, late).start()
            else:
                copy(near, late).start()

    @pl.when(z == 0)
    def _():
        for b in range(blocks):
            for c in range(n_tp - 1, 1, -1):
                right_copy(c, b).wait_send()
            if b == blocks - 2:
                send_some(1, right_copy, 1)
        send_rest(1, right_copy)

    @pl.when(z == n_tp - 1)
    def _():
        for b in range(blocks):
            for c in range(n_tp - 2):
                left_copy(c, b).wait_send()
            if b == blocks - 2:
                send_some(n_tp - 2, left_copy, -1)
        send_rest(n_tp - 2, left_copy)

    for n in range(given):
        @pl.when((chip == 0) & (z == 1))
        def _():
            side_second(1, n).wait_recv()
            side_third(1, recv_r, r_sem, n).start()

        @pl.when((chip == 0) & (z == n_tp - 2))
        def _():
            side_second(-1, n).wait_recv()
            side_third(n_tp - 2, recv_l, l_sem, n).start()

    chip_each(lambda copy: copy.wait_send())
    for d in range(1, hops + 1):
        @pl.when(i + 2 * d < n_loop)
        def _():
            id_chip(d).wait_send()

        @pl.when((core == 1) & (i >= 2 * d))
        def _():
            for copy in down_copies(d):
                copy.wait_send()

        @pl.when((core == 0) & (i >= 2 * d - 2))
        def _():
            for copy in up_copies(d - 1):
                copy.wait_send()

    for n in range(given):
        @pl.when((chip == 2) & (z == 0))
        def _():
            side_first(1, n).wait_send()

        @pl.when((chip == 2) & (z == n_tp - 1))
        def _():
            side_first(n_tp - 2, n).wait_send()

    def drain(b, carry):
        for c in range(n_tp):
            @pl.when(middle & (c > z))
            def _():
                right_copy(c, b).wait_send()

            @pl.when(middle & (c < z))
            def _():
                left_copy(c, b).wait_send()
        return carry

    lax.fori_loop(0, blocks, drain, 0)

    def finish(n, carry):
        b = lax.rem(n + given, blocks)
        rows = pl.ds(pl.multiple_of(b * ROWS, ROWS), ROWS)

        @pl.when(z == 0)
        def _():
            left_copy(z, b).wait_recv()
            out_ref[rows, :] = (part[z, rows, :].astype(jnp.float32)
                                + recv_l[z, rows, :].astype(jnp.float32)).astype(out_ref.dtype)

        @pl.when(z == n_tp - 1)
        def _():
            right_copy(z, b).wait_recv()
            out_ref[rows, :] = (part[z, rows, :].astype(jnp.float32)
                                + recv_r[z, rows, :].astype(jnp.float32)).astype(out_ref.dtype)

        @pl.when(middle)
        def _():
            right_copy(z, b).wait_recv()
            left_copy(z, b).wait_recv()
            out_ref[rows, :] = (part[z, rows, :].astype(jnp.float32)
                                + recv_r[z, rows, :].astype(jnp.float32)
                                + recv_l[z, rows, :].astype(jnp.float32)).astype(out_ref.dtype)
        return carry

    lax.fori_loop(0, blocks, finish, 0)

    def drain_late(b, carry):
        direct = (b >= given) | (chip != 2)

        @pl.when((z == 0) & direct)
        def _():
            right_copy(1, b).wait_send()

        @pl.when((z == n_tp - 1) & direct)
        def _():
            left_copy(n_tp - 2, b).wait_send()
        return carry

    lax.fori_loop(0, blocks, drain_late, 0)
    for n in range(given):
        @pl.when((chip == 0) & (z == 0))
        def _():
            side_second(1, n).wait_send()

        @pl.when((chip == 0) & (z == n_tp - 1))
        def _():
            side_second(-1, n).wait_send()

        @pl.when((chip == 0) & (z == 1))
        def _():
            side_third(1, recv_r, r_sem, n).wait_send()

        @pl.when((chip == 0) & (z == n_tp - 2))
        def _():
            side_third(n_tp - 2, recv_l, l_sem, n).wait_send()


def per_device(queries, key_values, prompt_ids, out_weight):
    n_loop, n_tp = lax.axis_size("loop"), lax.axis_size("tp")
    tok, q_cols = queries.shape
    depth, d_out = out_weight.shape
    width = d_out // n_tp
    reach = min(8, n_loop // 2)
    blocks = tok // ROWS
    hops = reach // 2
    vmem = pltpu.VMEM
    dma = pltpu.SemaphoreType.DMA
    any_spec = pl.BlockSpec(memory_space=pl.ANY)
    vmem_spec = pl.BlockSpec(memory_space=pltpu.VMEM)
    return pl.pallas_call(
        functools.partial(kernel, n_loop, n_tp, reach),
        out_shape=pltpu.VMEM((tok, width), jnp.bfloat16),
        in_specs=[any_spec] * 4,
        out_specs=vmem_spec,
        scratch_shapes=[
            vmem((tok, q_cols), jnp.bfloat16),
            vmem((reach + 1, tok, 2 * HD), jnp.bfloat16),
            vmem(((reach + 1) * tok, 2 * HD), jnp.bfloat16),
            vmem((reach + 1, 1, tok), jnp.int32),
            vmem((tok, 1), jnp.float32),
            vmem((ROWS, reach * tok), jnp.float32),
            vmem((ROWS, q_cols), jnp.bfloat16),
            vmem((depth, d_out), jnp.bfloat16),
            vmem((n_tp, tok, width), jnp.bfloat16),
            vmem((n_tp, tok, width), jnp.bfloat16),
            vmem((n_tp, tok, width), jnp.bfloat16),
            vmem((2, ROWS, width), jnp.bfloat16),
            vmem((2, ROWS, width), jnp.bfloat16),
            dma((3,)), dma((n_tp,)), dma((reach,)), dma((reach,)), dma((2, hops)), dma((2, hops)), dma((5, 2)),
            dma((reach,)), dma((reach,)),
            dma((n_tp, blocks)), dma((n_tp, blocks)), dma((n_tp, blocks)),
        ],
        compiler_params=pltpu.CompilerParams(
            collective_id=0, has_side_effects=True, vmem_limit_bytes=32 * 1024 * 1024),
        cost_estimate=pl.CostEstimate(flops=3_500_000_000, bytes_accessed=10_000_000, transcendentals=2_000_000),
    )(*(pltpu.with_memory_space_constraint(x, pltpu.HBM)
        for x in (queries, key_values, prompt_ids.reshape(1, tok), out_weight)))


def solution(mesh):
    in_specs = (P("loop", "tp"), P("loop", "tp"), P("loop"), P("tp", None))
    out_specs = P("loop", "tp")
    return jax.shard_map(
        per_device, mesh=mesh, in_specs=in_specs, out_specs=out_specs, check_vma=False
    )
```

```python
import functools
import math

import jax
import jax.numpy as jnp
from jax import lax
from jax.experimental import pallas as pl
from jax.experimental.pallas import tpu as pltpu
from jax.sharding import PartitionSpec as P

HD = 128
BLOCKED = -1e30
ROWS = 32
STACK = 8
MESH = pl.DeviceIdType.MESH


def kernel(n_loop, n_tp, reach, q_hbm, kv_hbm, ids_hbm, w_hbm, out_ref,
           q_ref, kv_buf, v_buf, id_buf, q_col, bias, attn, w_ref, part, recv_r, recv_l, side_a, side_b,
           load_sem, w_sem, kv_send, kv_recv, chip_send, chip_recv, side_sem, id_send, id_recv, send_sem, r_sem, l_sem):
    tok = q_ref.shape[0]
    heads = q_ref.shape[1] // HD
    width = part.shape[2]
    blocks = tok // ROWS
    far_last = reach * tok
    scale = math.log2(math.e) / math.sqrt(HD)
    i = lax.axis_index("loop")
    z = lax.axis_index("tp")

    load_q = pltpu.make_async_copy(q_hbm, q_ref, load_sem.at[0])
    load_kv = pltpu.make_async_copy(kv_hbm, kv_buf.at[reach], load_sem.at[1])
    low_half = z < n_tp // 2

    def load_w(j):
        c = jnp.where(low_half, n_tp - 1 - j, j)
        cols = pl.ds(pl.multiple_of(c * width, width), width)
        return pltpu.make_async_copy(w_hbm.at[:, cols], w_ref.at[:, cols], w_sem.at[j])

    load_ids = pltpu.make_async_copy(ids_hbm, id_buf.at[reach], load_sem.at[2])

    core = lax.rem(i, 2)
    chip = i // 2
    hops = reach // 2

    half = tok // 2

    def id_chip(d):
        return pltpu.make_async_remote_copy(
            src_ref=ids_hbm, dst_ref=id_buf.at[reach - 2 * d], send_sem=id_send.at[d - 1],
            recv_sem=id_recv.at[2 * d - 1], device_id=(i + 2 * d, z), device_id_type=MESH)

    def kv_chip(h, d):
        rows = pl.ds(h * half, half)
        return pltpu.make_async_remote_copy(
            src_ref=kv_hbm.at[rows], dst_ref=kv_buf.at[reach - 2 * d, rows],
            send_sem=chip_send.at[h, d - 1], recv_sem=chip_recv.at[h, d - 1],
            device_id=(i + 2 * d, z), device_id_type=MESH)

    def chip_each(act):
        for h in range(2):
            for d in range(hops, 0, -1):
                @pl.when(i + 2 * d < n_loop)
                def _():
                    act(kv_chip(h, d))

    def up_copies(d):
        return [
            pltpu.make_async_remote_copy(
                src_ref=source if d == 0 else target.at[reach - 2 * d], dst_ref=target.at[reach - 2 * d - 1],
                send_sem=sends.at[hops + d], recv_sem=arrivals.at[2 * d],
                device_id=(i + 1, z), device_id_type=MESH)
            for source, target, sends, arrivals in (
                (ids_hbm, id_buf, id_send, id_recv), (kv_hbm, kv_buf, kv_send, kv_recv))]

    def down_copies(d):
        return [
            pltpu.make_async_remote_copy(
                src_ref=target.at[reach - 2 * d], dst_ref=target.at[reach - 2 * d + 1],
                send_sem=sends.at[hops + d - 1], recv_sem=arrivals.at[2 * d - 2],
                device_id=(i - 1, z), device_id_type=MESH)
            for target, sends, arrivals in ((id_buf, id_send, id_recv), (kv_buf, kv_send, kv_recv))]

    def right_copy(c, b):
        rows = pl.ds(pl.multiple_of(b * ROWS, ROWS), ROWS)
        return pltpu.make_async_remote_copy(
            src_ref=part.at[c, rows], dst_ref=recv_r.at[c, rows], send_sem=send_sem.at[c, b],
            recv_sem=r_sem.at[c, b], device_id=(i, z + 1), device_id_type=MESH)

    def left_copy(c, b):
        rows = pl.ds(pl.multiple_of(b * ROWS, ROWS), ROWS)
        return pltpu.make_async_remote_copy(
            src_ref=part.at[c, rows], dst_ref=recv_l.at[c, rows], send_sem=send_sem.at[c, b],
            recv_sem=l_sem.at[c, b], device_id=(i, z - 1), device_id_type=MESH)

    side = n_loop == 8 and n_tp >= 4 and reach == 4
    given = 2 if side else 0

    def side_first(c, b):
        return pltpu.make_async_remote_copy(
            src_ref=part.at[c, pl.ds(b * ROWS, ROWS)], dst_ref=side_a.at[b], send_sem=side_sem.at[0, b],
            recv_sem=side_sem.at[1, b], device_id=(i - 4, z), device_id_type=MESH)

    def side_second(step, b):
        return pltpu.make_async_remote_copy(
            src_ref=side_a.at[b], dst_ref=side_b.at[b], send_sem=side_sem.at[2, b],
            recv_sem=side_sem.at[3, b], device_id=(i, z + step), device_id_type=MESH)

    def side_third(c, target, sems, b):
        return pltpu.make_async_remote_copy(
            src_ref=side_b.at[b], dst_ref=target.at[c, pl.ds(b * ROWS, ROWS)], send_sem=side_sem.at[4, b],
            recv_sem=sems.at[c, b], device_id=(i + 4, z), device_id_type=MESH)

    barrier = pltpu.get_barrier_semaphore()
    pl.semaphore_signal(barrier, inc=1, device_id=(i + 1 - 2 * core, z), device_id_type=MESH)
    for d in range(1, hops + 1):
        @pl.when(i + 2 * d < n_loop)
        def _():
            pl.semaphore_signal(barrier, inc=1, device_id=(i + 2 * d, z), device_id_type=MESH)

        @pl.when(i - 2 * d >= 0)
        def _():
            pl.semaphore_signal(barrier, inc=1, device_id=(i - 2 * d, z), device_id_type=MESH)

    @pl.when(z > 0)
    def _():
        pl.semaphore_signal(barrier, inc=1, device_id=(i, z - 1), device_id_type=MESH)

    @pl.when(z < n_tp - 1)
    def _():
        pl.semaphore_signal(barrier, inc=1, device_id=(i, z + 1), device_id_type=MESH)

    greeted = (1 + jnp.minimum(chip, hops) + jnp.minimum(n_loop // 2 - 1 - chip, hops)
               + jnp.minimum(z, 1) + jnp.minimum(n_tp - 1 - z, 1))
    load_ids.start()
    load_kv.start()
    load_q.start()
    for j in range(n_tp):
        load_w(j).start()
    pl.semaphore_wait(barrier, greeted)

    for d in range(1, hops + 1):
        @pl.when(i + 2 * d < n_loop)
        def _():
            id_chip(d).start()

    chip_each(lambda copy: copy.start())

    @pl.when(core == 0)
    def _():
        for copy in up_copies(0):
            copy.start()

    for k in range(1, reach + 1):
        @pl.when(i < k)
        def _():
            kv_buf[reach - k] = jnp.zeros(kv_buf.shape[1:], kv_buf.dtype)
            id_buf[reach - k] = jnp.full(id_buf.shape[1:], -1, id_buf.dtype)
    load_ids.wait()
    own_ids = id_buf[reach].astype(jnp.float32)
    square = (tok, tok)
    q_col[...] = jnp.max(
        jnp.where(lax.broadcasted_iota(jnp.int32, square, 0) == lax.broadcasted_iota(jnp.int32, square, 1),
                  jnp.broadcast_to(own_ids, square), -1.0), axis=1, keepdims=True)
    v_buf[:, HD:] = jnp.ones((v_buf.shape[0], HD), v_buf.dtype)
    load_kv.wait()
    load_q.wait()
    for d in range(hops, 0, -1):
        @pl.when(i >= 2 * d)
        def _():
            id_chip(d).wait_recv()
            kv_chip(0, d).wait_recv()
            kv_chip(1, d).wait_recv()

            @pl.when(core == 1)
            def _():
                for copy in down_copies(d):
                    copy.start()

            if d < hops:
                @pl.when(core == 0)
                def _():
                    for copy in up_copies(d):
                        copy.start()
    for d in range(1, hops + 1):
        @pl.when((core == 0) & (i >= 2 * d))
        def _():
            for copy in down_copies(d):
                copy.wait_recv()

        @pl.when((core == 1) & (i >= 2 * d - 1))
        def _():
            for copy in up_copies(d - 1):
                copy.wait_recv()
    for s in range(reach + 1):
        v_buf[s * tok:(s + 1) * tok, :HD] = kv_buf[s, :, HD:]

    def compute(b):
        rows = pl.ds(pl.multiple_of(b * ROWS, ROWS), ROWS)
        q_ids = q_col[rows, :]
        shape = (ROWS, tok)
        lower = (lax.broadcasted_iota(jnp.int32, shape, 1)
                 <= lax.broadcasted_iota(jnp.int32, shape, 0) + b * ROWS)
        key_ids = [jnp.broadcast_to(id_buf[s].astype(jnp.float32), shape) for s in range(reach + 1)]
        shared = jnp.where(lower, key_ids[reach], key_ids[0])
        for s, ids in enumerate([shared] + key_ids[1:reach]):
            bias[:, s * tok:(s + 1) * tok] = jnp.where(ids == q_ids, 0.0, BLOCKED)
        keys = kv_buf[:, :, :HD].reshape((reach + 1) * tok, HD)
        for h in range(0, heads, STACK):
            q = jnp.concatenate([q_ref[rows, (h + j) * HD:(h + j + 1) * HD] for j in range(STACK)], axis=0)
            s = lax.dot_general(q, keys, (((1,), (1,)), ((), ())), preferred_element_type=jnp.float32)
            s = s.reshape(STACK, ROWS, (reach + 1) * tok)
            s = jnp.concatenate(
                [jnp.where(lower[None], s[:, :, far_last:], s[:, :, :tok]), s[:, :, tok:far_last]], axis=2)
            s = s * scale + bias[...][None]
            p = jnp.exp2(s - jnp.max(s, axis=2, keepdims=True))
            first = p[:, :, :tok]
            p = jnp.concatenate(
                [jnp.where(lower[None], 0.0, first), p[:, :, tok:], jnp.where(lower[None], first, 0.0)], axis=2)
            p = p.reshape(STACK * ROWS, (reach + 1) * tok).astype(jnp.bfloat16)
            o = jnp.dot(p, v_buf[...], preferred_element_type=jnp.float32)
            o = (o[:, :HD] / o[:, HD:]).astype(jnp.bfloat16)
            for j in range(STACK):
                attn[:, (h + j) * HD:(h + j + 1) * HD] = o[j * ROWS:(j + 1) * ROWS]

        for j in range(n_tp):
            c = jnp.where(low_half, n_tp - 1 - j, j)

            @pl.when(b == 0)
            def _():
                load_w(j).wait()

            part[c, rows, :] = jnp.dot(
                attn[...], w_ref[:, pl.ds(pl.multiple_of(c * width, width), width)],
                preferred_element_type=jnp.float32).astype(jnp.bfloat16)

            @pl.when((z == 0) & (c >= 2))
            def _():
                right_copy(c, b).start()

            @pl.when((z == n_tp - 1) & (c < n_tp - 2))
            def _():
                left_copy(c, b).start()

        for n in range(given):
            @pl.when((b == n) & (chip == 2) & (z == 0))
            def _():
                side_first(1, n).start()

            @pl.when((b == n) & (chip == 2) & (z == n_tp - 1))
            def _():
                side_first(n_tp - 2, n).start()

    def forward_right(b):
        rows = pl.ds(pl.multiple_of(b * ROWS, ROWS), ROWS)
        for c in range(n_tp - 1, 1, -1):
            @pl.when(c > z)
            def _():
                copy = right_copy(c, b)
                copy.wait_recv()
                part[c, rows, :] = (part[c, rows, :].astype(jnp.float32)
                                    + recv_r[c, rows, :].astype(jnp.float32)).astype(jnp.bfloat16)
                copy.start()

    def forward_left(b):
        rows = pl.ds(pl.multiple_of(b * ROWS, ROWS), ROWS)
        for c in range(n_tp - 2):
            @pl.when(c < z)
            def _():
                copy = left_copy(c, b)
                copy.wait_recv()
                part[c, rows, :] = (part[c, rows, :].astype(jnp.float32)
                                    + recv_l[c, rows, :].astype(jnp.float32)).astype(jnp.bfloat16)
                copy.start()

    middle = jnp.logical_and(z > 0, z < n_tp - 1)

    def step(b, carry):
        @pl.when(b < blocks)
        def _():
            compute(b)

        right_b = b - jnp.where(low_half, 1, 2)
        left_b = b - jnp.where(low_half, 2, 1)

        @pl.when(middle & low_half & (right_b >= 0) & (right_b < blocks))
        def _():
            forward_right(right_b)

        @pl.when(middle & (left_b >= 0) & (left_b < blocks))
        def _():
            forward_left(left_b)

        @pl.when(middle & jnp.logical_not(low_half) & (right_b >= 0) & (right_b < blocks))
        def _():
            forward_right(right_b)
        return carry

    lax.fori_loop(0, blocks + 2, step, 0)

    def send_late(near, copy, step):
        for n in range(given):
            @pl.when(chip == 0)
            def _():
                side_first(near, n).wait_recv()
                side_second(step, n).start()

            @pl.when(chip != 2)
            def _():
                copy(near, n).start()
        for late in range(given, blocks):
            copy(near, late).start()

    @pl.when(z == 0)
    def _():
        for b in range(blocks):
            for c in range(n_tp - 1, 1, -1):
                right_copy(c, b).wait_send()
            if b == blocks - 2:
                send_late(1, right_copy, 1)

    @pl.when(z == n_tp - 1)
    def _():
        for b in range(blocks):
            for c in range(n_tp - 2):
                left_copy(c, b).wait_send()
            if b == blocks - 2:
                send_late(n_tp - 2, left_copy, -1)

    for n in range(given):
        @pl.when((chip == 0) & (z == 1))
        def _():
            side_second(1, n).wait_recv()
            side_third(1, recv_r, r_sem, n).start()

        @pl.when((chip == 0) & (z == n_tp - 2))
        def _():
            side_second(-1, n).wait_recv()
            side_third(n_tp - 2, recv_l, l_sem, n).start()

    chip_each(lambda copy: copy.wait_send())
    for d in range(1, hops + 1):
        @pl.when(i + 2 * d < n_loop)
        def _():
            id_chip(d).wait_send()

        @pl.when((core == 1) & (i >= 2 * d))
        def _():
            for copy in down_copies(d):
                copy.wait_send()

        @pl.when((core == 0) & (i >= 2 * d - 2))
        def _():
            for copy in up_copies(d - 1):
                copy.wait_send()

    for n in range(given):
        @pl.when((chip == 2) & (z == 0))
        def _():
            side_first(1, n).wait_send()

        @pl.when((chip == 2) & (z == n_tp - 1))
        def _():
            side_first(n_tp - 2, n).wait_send()

    def drain(b, carry):
        for c in range(n_tp):
            @pl.when(middle & (c > z))
            def _():
                right_copy(c, b).wait_send()

            @pl.when(middle & (c < z))
            def _():
                left_copy(c, b).wait_send()
        return carry

    lax.fori_loop(0, blocks, drain, 0)

    def finish(n, carry):
        b = lax.rem(n + given, blocks)
        rows = pl.ds(pl.multiple_of(b * ROWS, ROWS), ROWS)

        @pl.when(z == 0)
        def _():
            left_copy(z, b).wait_recv()
            out_ref[rows, :] = (part[z, rows, :].astype(jnp.float32)
                                + recv_l[z, rows, :].astype(jnp.float32)).astype(out_ref.dtype)

        @pl.when(z == n_tp - 1)
        def _():
            right_copy(z, b).wait_recv()
            out_ref[rows, :] = (part[z, rows, :].astype(jnp.float32)
                                + recv_r[z, rows, :].astype(jnp.float32)).astype(out_ref.dtype)

        @pl.when(middle)
        def _():
            right_copy(z, b).wait_recv()
            left_copy(z, b).wait_recv()
            out_ref[rows, :] = (part[z, rows, :].astype(jnp.float32)
                                + recv_r[z, rows, :].astype(jnp.float32)
                                + recv_l[z, rows, :].astype(jnp.float32)).astype(out_ref.dtype)
        return carry

    lax.fori_loop(0, blocks, finish, 0)

    def drain_late(b, carry):
        direct = (b >= given) | (chip != 2)

        @pl.when((z == 0) & direct)
        def _():
            right_copy(1, b).wait_send()

        @pl.when((z == n_tp - 1) & direct)
        def _():
            left_copy(n_tp - 2, b).wait_send()
        return carry

    lax.fori_loop(0, blocks, drain_late, 0)
    for n in range(given):
        @pl.when((chip == 0) & (z == 0))
        def _():
            side_second(1, n).wait_send()

        @pl.when((chip == 0) & (z == n_tp - 1))
        def _():
            side_second(-1, n).wait_send()

        @pl.when((chip == 0) & (z == 1))
        def _():
            side_third(1, recv_r, r_sem, n).wait_send()

        @pl.when((chip == 0) & (z == n_tp - 2))
        def _():
            side_third(n_tp - 2, recv_l, l_sem, n).wait_send()


def per_device(queries, key_values, prompt_ids, out_weight):
    n_loop, n_tp = lax.axis_size("loop"), lax.axis_size("tp")
    tok, q_cols = queries.shape
    depth, d_out = out_weight.shape
    width = d_out // n_tp
    reach = min(8, n_loop // 2)
    blocks = tok // ROWS
    hops = reach // 2
    vmem = pltpu.VMEM
    dma = pltpu.SemaphoreType.DMA
    any_spec = pl.BlockSpec(memory_space=pl.ANY)
    vmem_spec = pl.BlockSpec(memory_space=pltpu.VMEM)
    return pl.pallas_call(
        functools.partial(kernel, n_loop, n_tp, reach),
        out_shape=pltpu.VMEM((tok, width), jnp.bfloat16),
        in_specs=[any_spec] * 4,
        out_specs=vmem_spec,
        scratch_shapes=[
            vmem((tok, q_cols), jnp.bfloat16),
            vmem((reach + 1, tok, 2 * HD), jnp.bfloat16),
            vmem(((reach + 1) * tok, 2 * HD), jnp.bfloat16),
            vmem((reach + 1, 1, tok), jnp.int32),
            vmem((tok, 1), jnp.float32),
            vmem((ROWS, reach * tok), jnp.float32),
            vmem((ROWS, q_cols), jnp.bfloat16),
            vmem((depth, d_out), jnp.bfloat16),
            vmem((n_tp, tok, width), jnp.bfloat16),
            vmem((n_tp, tok, width), jnp.bfloat16),
            vmem((n_tp, tok, width), jnp.bfloat16),
            vmem((2, ROWS, width), jnp.bfloat16),
            vmem((2, ROWS, width), jnp.bfloat16),
            dma((3,)), dma((n_tp,)), dma((reach,)), dma((reach,)), dma((2, hops)), dma((2, hops)), dma((5, 2)),
            dma((reach,)), dma((reach,)),
            dma((n_tp, blocks)), dma((n_tp, blocks)), dma((n_tp, blocks)),
        ],
        compiler_params=pltpu.CompilerParams(
            collective_id=0, has_side_effects=True, vmem_limit_bytes=32 * 1024 * 1024),
        cost_estimate=pl.CostEstimate(flops=3_500_000_000, bytes_accessed=10_000_000, transcendentals=2_000_000),
    )(*(pltpu.with_memory_space_constraint(x, pltpu.HBM)
        for x in (queries, key_values, prompt_ids.reshape(1, tok), out_weight)))


def solution(mesh):
    in_specs = (P("loop", "tp"), P("loop", "tp"), P("loop"), P("tp", None))
    out_specs = P("loop", "tp")
    return jax.shard_map(
        per_device, mesh=mesh, in_specs=in_specs, out_specs=out_specs, check_vma=False
    )
```
